32 devices in a mesh: pool: 8 (over y, x, core), head: 4 (over z).
Axes of the slice: x: 2, y: 2, z: 4, core: 2. Of those that a mesh axis runs over, the one named last changes fastest.
Arguments:
- x_rows: bfloat16 [256, 4096], P('pool'), may hold values from -3 to 3
- query: bfloat16 [256, 4096], P('pool', 'head'), may hold values from -170 to 170
- key_cache: bfloat16 [256, 4, 512, 128], P('pool', 'head'), may hold values from -6 to 6
- value_cache: bfloat16 [256, 4, 512, 128], P('pool', 'head'), may hold values from -6 to 6
- new_key: bfloat16 [256, 512], P('pool', 'head'), may hold values from -6 to 6
- new_value: bfloat16 [256, 512], P('pool', 'head'), may hold values from -6 to 6
- lengths: int32 [256], P('pool'), may hold values from 2 to 512, as said below
- out_proj: bfloat16 [4096, 4096], P('head'), may hold values from -0.5 to 0.5
- norm_gain: float32 [4096], replicated, may hold values from 0.5 to 1.5
- expert_ids: int32 [256, 8], P('pool'), may hold values from 0 to 15, all different within a row; in each aligned block of 32 rows (0 to 31, 32 to 63, ...) at most 32 rows name the same one
- gate_weights: float32 [256, 8], P('pool'), may hold values from 0.05 to 1
- w_gate: bfloat16 [16, 4096, 1024], P('pool', None, 'head'), may hold values from -0.09375 to 0.09375
- w_up: bfloat16 [16, 4096, 1024], P('pool', None, 'head'), may hold values from -0.09375 to 0.09375
- w_down: bfloat16 [16, 1024, 4096], P('pool', 'head'), may hold values from -0.1875 to 0.1875
Outputs:
- layer_out: bfloat16 [256, 4096], P('pool', 'head')
The draws below stay inside these ranges and needn't reach their ends.
Inputs may be any that keep to these rules, and one draw needn't show every extreme that they name: `expert_ids`: within the 32 requests of one index of pool, no expert is named by more than 32 pairs, a bound that some block reaches. `lengths`: request 0 uses all 512 slots.
All inputs are finite; a program needn't handle non-finite values.
Results may differ from the reference program's by a relative error of at most 0.017.
Values may be sent and summed in bfloat16 or wider, within the bound.
A program may use at most 128 MiB of HBM per device.

```python
import math
import jax
import jax.numpy as jnp
import numpy as np
from jax import lax

D = 4096
HD = 128
KVH = 4
QPK = 8
EFF = 1024
TOP = 8
CTX = 512
REQ_DEV = 32
REQS = 256
EXPERTS = 16
CAP = 32
MOST = 256


def cache_base(key):
    return jnp.clip(jax.random.normal(jax.random.fold_in(key, 101), (REQS, KVH, CTX, HD), jnp.float32), -6.0, 6.0)


def draw_key_cache(key, part):
    base_keys = cache_base(key)
    return base_keys.astype(jnp.bfloat16)


def draw_query(key, part):
    entries = jnp.clip(jax.random.normal(jax.random.fold_in(key, 202), (REQS, KVH, QPK, HD), jnp.float32), -6.0, 6.0)
    return entries.reshape(REQS, KVH * QPK * HD).astype(jnp.bfloat16)


def draw_lengths(key, part):
    drawn = jax.random.randint(jax.random.fold_in(key, 303), (REQS,), 2, CTX + 1, jnp.int32)
    return drawn.at[0].set(CTX)


def block_scale(own_key, dims, cuts, smallest, top_value):
    factor_of, own = 1.0, jax.random.fold_in(own_key, 6)
    for position, blocks in cuts:
        steps = jnp.exp(jax.random.uniform(jax.random.fold_in(own, position), (blocks,), jnp.float32, smallest / len(cuts), top_value / len(cuts)))
        factor_of = factor_of * jnp.repeat(steps, dims[position] // blocks).reshape([-1 if axis == position else 1 for axis in range(len(dims))])
    return factor_of


def deal_out(stream_key, own, number, rows, count, top, bound, skew):
    ranking = jax.random.permutation(stream_key, count)
    crowded, ordinary = portions_of(count, rows * top, bound, skew, True), portions_of(count, rows * top, bound, skew, False)
    places = jnp.arange(count)

    def named(sizes, turn):
        used = int((sizes > 0).sum())
        fixed = max(1, used // 4)
        shifted = fixed + (places - fixed + turn * (used - fixed)) % max(1, count - fixed)
        return jnp.zeros((count,), jnp.int32).at[ranking[jnp.where(places < fixed, places, shifted)]].set(jnp.asarray(sizes, jnp.int32))

    sizes = jnp.where(number % 4 == 0, named(crowded, number // 4), named(ordinary, number - number // 4 - 1))
    mixed = jax.random.permutation(jax.random.fold_in(own, 3), count)
    donor, receiver = mixed[0:count // 2 * 2:2], mixed[1:count // 2 * 2:2]
    room = jnp.minimum(sizes[donor] - 1, bound - sizes[receiver]) // 2
    room = jnp.where((donor == ranking[0]) | (receiver == ranking[0]) | (sizes[receiver] == 0), 0, jnp.maximum(room, 0))
    shifted = jax.random.randint(jax.random.fold_in(own, 4), (count // 2,), 0, 1 << 20) % (room + 1)
    sizes = sizes.at[donor].add(-shifted).at[receiver].add(shifted)
    members = jnp.searchsorted(jnp.cumsum(sizes), jnp.arange(rows * top), side="right").astype(jnp.int32)
    grid = members.reshape(top, rows).T
    grid = grid[jax.random.permutation(jax.random.fold_in(own, 1), rows)]
    turn = jax.random.randint(jax.random.fold_in(own, 2), (rows, 1), 0, top)
    return jnp.take_along_axis(grid, (jnp.arange(top)[None, :] + turn) % top, axis=1)


def portions_of(number_of, total, bound, slope, full):
    weights = [(1 << 20) // math.isqrt(rank ** slope) + 1 for rank in range(1, number_of + 1)]
    largest = bound if full else min(bound, max(-(-total // number_of), total * weights[0] // sum(weights)))
    least = 1 if total - largest >= number_of - 1 else 0
    holding, spare = [largest] + [least] * (number_of - 1), total - largest - least * (number_of - 1)
    while spare > 0:
        free = [i for i in range(1, number_of) if holding[i] < largest] or [i for i in range(1, number_of) if holding[i] < bound]
        mass, budget = sum([weights[i] for i in free]), spare
        for i in free:
            more = min(bound - holding[i], max(1, budget * weights[i] // mass), spare)
            holding[i] = holding[i] + more
            spare = spare - more
    return np.array(holding)


def bell_draw(rng, dims, deviation, limit, cuts=(), kind=jnp.bfloat16):
    factor_of = block_scale(rng, dims, cuts, -0.22, 0.18) if cuts else 1.0
    array = jax.random.normal(rng, dims, jnp.float32) * deviation * factor_of
    return jnp.minimum(jnp.maximum(array, -limit), limit).astype(kind)


def setup_inputs(seed: int = 0) -> dict:
    keys = jax.random.split(jax.random.key(seed), 15)
    x_rows = bell_draw(keys[0], (REQS, D), 0.5, 3.0, ((0, 8),))
    query = draw_query(jax.random.fold_in(keys[14], 71), 0)
    key_cache = draw_key_cache(jax.random.fold_in(keys[14], 71), 0)
    value_cache = bell_draw(keys[3], (REQS, KVH, CTX, HD), 1.0, 6.0, ((0, 8), (1, 4)))
    new_key = bell_draw(keys[4], (REQS, KVH * HD), 1.0, 6.0, ((0, 8), (1, 4)))
    new_value = bell_draw(keys[5], (REQS, KVH * HD), 1.0, 6.0, ((0, 8), (1, 4)))
    lengths = draw_lengths(jax.random.fold_in(keys[14], 71), 0)
    out_proj = bell_draw(keys[7], (KVH * QPK * HD, D), HD ** -0.5, 0.5, ((0, 4),))
    norm_gain = jnp.clip(1.0 + 0.1 * jax.random.normal(keys[8], (D,), jnp.float32), 0.5, 1.5)
    expert_ids_keys = jax.random.split(jax.random.fold_in(keys[9], 1), REQS // REQ_DEV)
    expert_ids_turns = jax.random.permutation(jax.random.fold_in(keys[9], 3), REQS // REQ_DEV)
    expert_ids = jax.vmap(lambda own, number: deal_out(jax.random.fold_in(keys[9], 2), own, number, REQ_DEV, EXPERTS, TOP, CAP, 2))(expert_ids_keys, expert_ids_turns).reshape((REQS, TOP))
    gate_weights = jnp.clip(jnp.exp(math.log(1.0) - 2.9957323 * jax.random.uniform(keys[10], (REQS, TOP), jnp.float32) ** block_scale(keys[10], (REQS, TOP), ((0, 8),), -0.2, 0.2)), 0.05, 1.0)
    w_gate = bell_draw(keys[11], (EXPERTS, D, EFF), D ** -0.5, 0.09375, ((0, 8), (2, 4)))
    w_up = bell_draw(keys[12], (EXPERTS, D, EFF), D ** -0.5, 0.09375, ((0, 8), (2, 4)))
    w_down = bell_draw(keys[13], (EXPERTS, EFF, D), EFF ** -0.5, 0.1875, ((0, 8), (1, 4)))
    return {"x_rows": x_rows, "query": query, "key_cache": key_cache, "value_cache": value_cache, "new_key": new_key, "new_value": new_value, "lengths": lengths, "out_proj": out_proj, "norm_gain": norm_gain, "expert_ids": expert_ids, "gate_weights": gate_weights, "w_gate": w_gate, "w_up": w_up, "w_down": w_down}


def reference(x_rows, query, key_cache, value_cache, new_key, new_value, lengths, out_proj, norm_gain, expert_ids, gate_weights, w_gate, w_up, w_down):
    score_scale = HD ** (-0.5)
    queries = query.reshape(REQS, KVH, QPK, HD).astype(jnp.float32)
    cached_keys = key_cache.astype(jnp.float32)
    cached_values = value_cache.astype(jnp.float32)
    scores = jnp.einsum('rhqd,rhcd->rhqc', queries, cached_keys) * score_scale
    fresh_score = jnp.einsum('rhqd,rhd->rhq', queries, new_key.reshape(REQS, KVH, HD).astype(jnp.float32)) * score_scale
    live_mask = (jnp.arange(CTX)[None, :] < lengths[:, None])[:, None, None, :]
    scores = jnp.where(live_mask, scores, -1e+30)
    highest = jnp.maximum(lax.optimization_barrier(jnp.max(scores, -1)), fresh_score)
    weights = jnp.where(live_mask, jnp.exp(scores - highest[..., None]), 0.0)
    own_term = jnp.exp(fresh_score - highest)
    totals = lax.optimization_barrier(jnp.sum(weights, -1)) + own_term
    probs = lax.optimization_barrier((weights / totals[..., None]).astype(jnp.bfloat16)).astype(jnp.float32)
    own_prob = lax.optimization_barrier((own_term / totals).astype(jnp.bfloat16)).astype(jnp.float32)
    mixed = jnp.einsum('rhqc,rhcd->rhqd', probs, cached_values)
    mixed = mixed + own_prob[..., None] * new_value.reshape(REQS, KVH, 1, HD).astype(jnp.float32)
    attn = mixed.astype(jnp.bfloat16).reshape(REQS, KVH * QPK * HD)
    hidden = x_rows.astype(jnp.float32) + jnp.dot(attn, out_proj, preferred_element_type=jnp.float32)
    mean_square = lax.optimization_barrier(jnp.mean(hidden * hidden, -1, keepdims=True))
    normed = (hidden * lax.rsqrt(mean_square + 1e-06) * norm_gain.astype(jnp.float32)[None, :]).astype(jnp.bfloat16)

    def one_expert(moe_sum, bundle):
        gate_mat, up_mat, down_mat, expert_index = bundle
        chosen_pair = expert_ids == expert_index
        chosen_row = jnp.any(chosen_pair, -1)
        row_weight = lax.optimization_barrier(jnp.sum(jnp.where(chosen_pair, gate_weights, 0.0), -1))
        picked_rows = jnp.nonzero(chosen_row, size=MOST, fill_value=0)[0].astype(jnp.int32)
        valid_rows = jnp.arange(MOST) < jnp.sum(chosen_row.astype(jnp.int32))
        picked = normed[picked_rows]
        gate_part = jnp.dot(picked, gate_mat, preferred_element_type=jnp.float32)
        up_part = jnp.dot(picked, up_mat, preferred_element_type=jnp.float32)
        act = (jax.nn.silu(gate_part) * up_part).astype(jnp.bfloat16)
        produced = lax.optimization_barrier(jnp.dot(act, down_mat, preferred_element_type=jnp.float32).astype(jnp.bfloat16)).astype(jnp.float32)
        scaled = produced * jnp.where(valid_rows, row_weight[picked_rows], 0.0)[:, None]
        return (moe_sum.at[picked_rows].add(scaled), None)
    start = jnp.zeros((REQS, D), jnp.float32)
    moe_sum, unused = lax.scan(one_expert, start, (w_gate, w_up, w_down, jnp.arange(EXPERTS).astype(jnp.int32)))
    return (hidden + moe_sum).astype(jnp.bfloat16)
```

```python
import functools

import jax
import jax.numpy as jnp
from jax import lax
from jax.experimental import pallas as pl
from jax.experimental.pallas import tpu as pltpu
from jax.sharding import PartitionSpec as P

VMEM_BYTES = 60 * 1024 * 1024


def attend(query, key_cache, value_cache, new_key, new_value, lengths):
    token_count = query.shape[0]
    head_size = new_key.shape[1]
    queries = query.reshape(token_count, -1, head_size)
    cached_keys = key_cache[:, 0]
    cached_values = value_cache[:, 0]
    score_scale = head_size ** (-0.5)
    scores = (
        jnp.einsum("rqd,rcd->rqc", queries, cached_keys, preferred_element_type=jnp.float32)
        * score_scale
    )
    fresh_score = (
        jnp.einsum("rqd,rd->rq", queries, new_key, preferred_element_type=jnp.float32) * score_scale
    )
    live_mask = (jnp.arange(cached_keys.shape[1])[None, :] < lengths[:, None])[:, None, :]
    scores = jnp.where(live_mask, scores, -1e30)
    highest = jnp.maximum(jnp.max(scores, -1), fresh_score)
    weights = jnp.where(live_mask, jnp.exp(scores - highest[..., None]), 0.0)
    own_term = jnp.exp(fresh_score - highest)
    totals = jnp.sum(weights, -1) + own_term
    probs = (weights / totals[..., None]).astype(jnp.bfloat16)
    own_prob = (own_term / totals).astype(jnp.bfloat16)
    mixed = jnp.einsum("rqc,rcd->rqd", probs, cached_values, preferred_element_type=jnp.float32)
    mixed = (
        mixed + own_prob.astype(jnp.float32)[..., None] * new_value.astype(jnp.float32)[:, None, :]
    )
    return mixed.astype(jnp.bfloat16).reshape(token_count, -1)


MESH = pl.DeviceIdType.MESH
F32 = jnp.float32
BF16 = jnp.bfloat16


def flip(index, offset, count):
    result, bit = 0, 1
    while bit < count:
        result = result + bit * ((index // bit + offset // bit) % 2)
        bit *= 2
    return result


def layer_kernel(
    pools,
    groups,
    experts,
    attn_ref,
    x_ref,
    gates_ref,
    gain_ref,
    proj_hbm,
    gate_hbm,
    up_hbm,
    down_hbm,
    out_ref,
    proj,
    gate,
    up,
    down,
    part_send,
    part_recv,
    hidden,
    slabs,
    rows_all,
    act,
    produced,
    pair_recv,
    plane_send,
    plane_recv,
    last_send,
    last_recv,
    load_sem,
    part_sems,
    slab_sems,
    gather_sems,
    pair_sems,
    swap_sems,
    plane_sems,
    last_sems,
):
    chips = pools // 2
    rows, share = hidden.shape
    width = groups * share
    local = gate.shape[0]
    units = gate.shape[3]
    pool, head = lax.axis_index("pool"), lax.axis_index("head")
    chip, core = pool // 2, pool % 2
    partner = {"pool": chip * 2 + 1 - core}
    above = [{"head": (head + k) % groups} for k in range(groups)]
    across = [{"pool": flip(chip, q, chips) * 2 + core} for q in range(chips)]
    order = list(range(1, groups)) + [0]

    def send(source, target, sems, place, device):
        copy = pltpu.make_async_remote_copy(
            src_ref=source,
            dst_ref=target,
            send_sem=sems.at[(0,) + place],
            recv_sem=sems.at[(1,) + place],
            device_id=device,
            device_id_type=MESH,
        )
        copy.start()
        return copy

    loads = {}

    def load(name, index, source, target):
        copy = pltpu.make_async_copy(source, target, load_sem.at[len(loads)])
        copy.start()
        loads[name, index] = copy

    def columns(k):
        return pl.ds(pl.multiple_of((head + k) % groups * share, share), share)

    def depths(k):
        return pl.ds(pl.multiple_of((head - k + groups) % groups * share, share), share)

    for k in order:
        load("proj", k, proj_hbm.at[:, columns(k)], proj.at[k])
    for k in range(groups):
        for e in range(local):
            load("gate", (e, k), gate_hbm.at[e, depths(k)], gate.at[e, k])
            load("up", (e, k), up_hbm.at[e, depths(k)], up.at[e, k])
    for k in order:
        for e in range(local):
            load("down", (e, k), down_hbm.at[e, :, columns(k)], down.at[k, e])

    barrier = pltpu.get_barrier_semaphore()
    greeted = above[1:] + across[1:] + [partner]
    for device in greeted:
        pl.semaphore_signal(barrier, inc=1, device_id=device, device_id_type=MESH)
    pl.semaphore_wait(barrier, len(greeted))

    sent = []

    parts = {}
    for k in order:
        loads["proj", k].wait()
        term = jnp.dot(attn_ref[...], proj[k], preferred_element_type=F32)
        if k:
            part_send[k] = term.astype(BF16)
            parts[k] = send(part_send.at[k], part_recv.at[k], part_sems, (k,), above[k])
        else:
            own = pl.ds(pl.multiple_of(head * share, share), share)
            hidden[...] = term + x_ref[:, own].astype(F32)
    total = hidden[...]
    for k in order[:-1]:
        parts[k].wait_recv()
        total = total + part_recv[k].astype(F32)
    hidden[...] = total
    slabs[0] = total.astype(BF16)

    shared = {k: send(slabs.at[0], slabs.at[k], slab_sems, (k,), above[k]) for k in order[:-1]}
    for k in order[:-1]:
        shared[k].wait_recv()
    squares = jnp.zeros((rows, 1), F32)
    for k in range(groups):
        value = slabs[k].astype(F32)
        squares = squares + jnp.sum(value * value, -1, keepdims=True)
    scale = lax.rsqrt(squares / width + 1e-06)
    for k in range(groups):
        slab_gain = gain_ref[(head - k + groups) % groups]
        rows_all[0, :, k * share : (k + 1) * share] = (
            slabs[k].astype(F32) * scale * slab_gain
        ).astype(BF16)
    rows_all[0, :, width:] = gates_ref[...]

    gathers = {
        q: send(rows_all.at[0], rows_all.at[q], gather_sems, (q,), across[q])
        for q in range(1, chips)
    }
    pairs = [send(rows_all.at[0], rows_all.at[chips], pair_sems, (0,), partner)]
    for q in range(1, chips):
        gathers[q].wait_recv()
        pairs.append(
            send(rows_all.at[q], rows_all.at[chips + q], pair_sems, (q,), partner)
        )
    for copy in pairs:
        copy.wait_recv()

    block = min(8, pools)
    for name in ("gate", "up"):
        for k in range(groups):
            for e in range(local):
                loads[name, (e, k)].wait()

    def expert_rows(index, carry):
        place = pl.ds(index * block, block)
        gates = rows_all[place, :, width:].reshape(block * rows, -1).astype(F32)
        lane = lax.broadcasted_iota(jnp.int32, gates.shape, 1)
        for e in range(local):
            gate_part = jnp.zeros((block * rows, units), F32)
            up_part = jnp.zeros((block * rows, units), F32)
            for k in range(groups):
                piece = rows_all[place, :, k * share : (k + 1) * share].reshape(
                    block * rows, share
                )
                gate_part += jnp.dot(piece, gate[e, k], preferred_element_type=F32)
                up_part += jnp.dot(piece, up[e, k], preferred_element_type=F32)
            expert = pool * local + e
            chosen = (lane == expert) | (lane == experts + expert)
            weight = jnp.sum(jnp.where(chosen, gates, 0.0), -1, keepdims=True)
            value = gate_part / (1.0 + jnp.exp(-gate_part)) * up_part * weight
            act[place, :, e * units : (e + 1) * units] = value.astype(BF16).reshape(
                block, rows, units
            )
        return carry

    lax.fori_loop(0, pools // block, expert_rows, 0)

    swaps, planes, lasts = {}, {}, {}

    def project(k):
        for e in range(local):
            loads["down", (e, k)].wait()

        def down_rows(index, carry):
            place = pl.ds(index * block, block)
            value = jnp.dot(
                act[place].reshape(block * rows, local * units),
                down[k].reshape(local * units, share),
                preferred_element_type=F32,
            )
            produced[k, place] = value.astype(BF16).reshape(block, rows, share)
            return carry

        lax.fori_loop(0, pools // block, down_rows, 0)
        swaps[k] = send(
            produced.at[k, pl.ds(chips, chips)], pair_recv.at[k], swap_sems, (k,), partner
        )

    def cross(k):
        swaps[k].wait_recv()
        for q in range(1, chips):
            plane_send[k, q] = (
                produced[k, q].astype(F32) + pair_recv[k, q].astype(F32)
            ).astype(BF16)
            planes[k, q] = send(
                plane_send.at[k, q], plane_recv.at[k, q], plane_sems, (k, q), across[q]
            )

    def finish(k):
        value = produced[k, 0].astype(F32) + pair_recv[k, 0].astype(F32)
        for q in range(1, chips):
            planes[k, q].wait_recv()
            value = value + plane_recv[k, q].astype(F32)
        if k:
            last_send[k] = value.astype(BF16)
            lasts[k] = send(last_send.at[k], last_recv.at[k], last_sems, (k,), above[k])
        else:
            value = value + hidden[...]
            for j in order[:-1]:
                lasts[j].wait_recv()
                value = value + last_recv[j].astype(F32)
            out_ref[...] = value.astype(BF16)

    for step in range(groups + 2):
        if step < groups:
            project(order[step])
        if 1 <= step <= groups:
            cross(order[step - 1])
        if step >= 2:
            finish(order[step - 2])

    for group in (parts, shared, gathers, swaps, planes, lasts):
        for copy in group.values():
            copy.wait_send()
    for copy in pairs:
        copy.wait_send()


def gate_table(expert_ids, gate_weights, experts):
    matching = expert_ids[:, :, None] == jnp.arange(experts)[None, None, :]
    table = jnp.sum(jnp.where(matching, gate_weights[:, :, None], 0.0), 1)
    first = lax.reduce_precision(table, 8, 7)
    rest = table - first
    lanes = -(-2 * experts // 128) * 128
    both = jnp.concatenate([first, rest], 1).astype(BF16)
    return jnp.pad(both, ((0, 0), (0, lanes - 2 * experts)))


def body(
    x_rows,
    query,
    key_cache,
    value_cache,
    new_key,
    new_value,
    lengths,
    out_proj,
    norm_gain,
    expert_ids,
    gate_weights,
    w_gate,
    w_up,
    w_down,
):
    pools = lax.axis_size("pool")
    groups = lax.axis_size("head")
    rows, width = x_rows.shape
    share = width // groups
    local, _, units = w_gate.shape
    experts = pools * local
    chips = pools // 2
    attn = attend(query, key_cache, value_cache, new_key, new_value, lengths)
    gates = gate_table(expert_ids, gate_weights, experts)
    lanes = gates.shape[1]
    depth = out_proj.shape[0]
    in_vmem = pl.BlockSpec(memory_space=pltpu.VMEM)
    in_hbm = pl.BlockSpec(memory_space=pl.ANY)
    dma = pltpu.SemaphoreType.DMA
    return pl.pallas_call(
        functools.partial(layer_kernel, pools, groups, experts),
        out_shape=jax.ShapeDtypeStruct((rows, share), BF16),
        in_specs=[in_vmem] * 4 + [in_hbm] * 4,
        out_specs=in_vmem,
        scratch_shapes=[
            pltpu.VMEM((groups, depth, share), BF16),
            pltpu.VMEM((local, groups, share, units), BF16),
            pltpu.VMEM((local, groups, share, units), BF16),
            pltpu.VMEM((groups, local, units, share), BF16),
            pltpu.VMEM((groups, rows, share), BF16),
            pltpu.VMEM((groups, rows, share), BF16),
            pltpu.VMEM((rows, share), F32),
            pltpu.VMEM((groups, rows, share), BF16),
            pltpu.VMEM((pools, rows, width + lanes), BF16),
            pltpu.VMEM((pools, rows, local * units), BF16),
            pltpu.VMEM((groups, pools, rows, share), BF16),
            pltpu.VMEM((groups, chips, rows, share), BF16),
            pltpu.VMEM((groups, chips, rows, share), BF16),
            pltpu.VMEM((groups, chips, rows, share), BF16),
            pltpu.VMEM((groups, rows, share), BF16),
            pltpu.VMEM((groups, rows, share), BF16),
            dma((groups * (1 + 3 * local),)),
            dma((2, groups)),
            dma((2, groups)),
            dma((2, chips)),
            dma((2, chips)),
            dma((2, groups)),
            dma((2, groups, chips)),
            dma((2, groups)),
        ],
        compiler_params=pltpu.CompilerParams(
            collective_id=0, has_side_effects=True, vmem_limit_bytes=VMEM_BYTES
        ),
    )(
        attn,
        x_rows,
        gates,
        norm_gain.reshape(groups, 1, share),
        out_proj,
        w_gate,
        w_up,
        w_down,
    )


def solution(mesh):
    placed = (
        P("pool", None),
        P("pool", "head"),
        P("pool", "head", None, None),
        P("pool", "head", None, None),
        P("pool", "head"),
        P("pool", "head"),
        P("pool"),
        P("head", None),
        P(),
        P("pool", None),
        P("pool", None),
        P("pool", None, "head"),
        P("pool", None, "head"),
        P("pool", "head", None),
    )
    return jax.shard_map(
        body, mesh=mesh, in_specs=placed, out_specs=P("pool", "head"), check_vma=False
    )
```

```python
import functools

import jax
import jax.numpy as jnp
from jax import lax
from jax.experimental import pallas as pl
from jax.experimental.pallas import tpu as pltpu
from jax.sharding import PartitionSpec as P

VMEM_BYTES = 60 * 1024 * 1024
HALVES = 2
TOGETHER = 8

MESH = pl.DeviceIdType.MESH
F32 = jnp.float32
BF16 = jnp.bfloat16


def flip(index, offset, count):
    result, bit = 0, 1
    while bit < count:
        result = result + bit * ((index // bit + offset // bit) % 2)
        bit *= 2
    return result


def layer_kernel(
    pools,
    groups,
    experts,
    lengths_ref,
    query_ref,
    new_key_ref,
    new_value_ref,
    x_ref,
    ids_ref,
    gate_weight_ref,
    gain_ref,
    key_hbm,
    value_hbm,
    proj_hbm,
    gate_hbm,
    up_hbm,
    down_hbm,
    out_ref,
    keys,
    values,
    query_heads,
    mixed_heads,
    fresh_keys,
    fresh_values,
    attn,
    proj,
    gate,
    up,
    down,
    part_send,
    part_recv,
    hidden,
    slabs,
    rows_all,
    act,
    produced,
    pair_recv,
    plane_recv,
    last_send,
    last_recv,
    cache_sem,
    load_sem,
    part_sems,
    slab_sems,
    gather_sems,
    pair_sems,
    swap_sems,
    plane_sems,
    last_sems,
):
    chips = pools // 2
    half, share = hidden.shape[1:]
    width = groups * share
    local = gate.shape[0]
    units = gate.shape[3]
    lanes = rows_all.shape[3] - width
    heads, head_size = query_heads.shape[1:]
    slots = keys.shape[1]
    pool, head = lax.axis_index("pool"), lax.axis_index("head")
    chip, core = pool // 2, pool % 2
    partner = {"pool": chip * 2 + 1 - core}
    above = [{"head": (head + k) % groups} for k in range(groups)]
    across = [{"pool": flip(chip, q, chips) * 2 + core} for q in range(chips)]
    order = list(range(1, groups)) + [0]
    sent = []

    def send(source, target, sems, place, device):
        copy = pltpu.make_async_remote_copy(
            src_ref=source,
            dst_ref=target,
            send_sem=sems.at[(0,) + place],
            recv_sem=sems.at[(1,) + place],
            device_id=device,
            device_id_type=MESH,
        )
        copy.start()
        sent.append(copy)
        return copy

    loads = {}

    def load(name, index, source, target):
        copy = pltpu.make_async_copy(source, target, load_sem.at[len(loads)])
        copy.start()
        loads[name, index] = copy

    def columns(k):
        return pl.ds(pl.multiple_of((head + k) % groups * share, share), share)

    def depths(k):
        return pl.ds(pl.multiple_of((head - k + groups) % groups * share, share), share)

    def cache_copies(index):
        place = pl.ds(index * TOGETHER, TOGETHER)
        return [
            pltpu.make_async_copy(key_hbm.at[place, 0], keys.at[place], cache_sem.at[0, index]),
            pltpu.make_async_copy(
                value_hbm.at[place, 0], values.at[place], cache_sem.at[1, index]
            ),
        ]

    blocks = half // TOGETHER

    def load_cache(a):
        for index in range(a * blocks, (a + 1) * blocks):
            for copy in cache_copies(index):
                copy.start()

    load_cache(0)
    for k in order:
        load("proj", k, proj_hbm.at[:, columns(k)], proj.at[k])
    for a in range(1, HALVES):
        load_cache(a)
    for k in range(groups):
        for e in range(local):
            load("gate", (e, k), gate_hbm.at[e, depths(k)], gate.at[e, k])
            load("up", (e, k), up_hbm.at[e, depths(k)], up.at[e, k])
    for k in order:
        for e in range(local):
            load("down", (e, k), down_hbm.at[e, :, columns(k)], down.at[k, e])

    barrier = pltpu.get_barrier_semaphore()
    greeted = above[1:] + across[1:] + [partner]
    for device in greeted:
        pl.semaphore_signal(barrier, inc=1, device_id=device, device_id_type=MESH)

    for i in range(heads):
        query_heads[:, i, :] = query_ref[:, i * head_size : (i + 1) * head_size].astype(F32)
    fresh_keys[...] = new_key_ref[...].astype(F32)
    fresh_values[...] = new_value_ref[...].astype(F32)
    score_scale = head_size ** (-0.5)

    def attend(a):
        def requests(index, carry):
            for copy in cache_copies(index):
                copy.wait()
            place = lax.broadcasted_iota(jnp.int32, (heads, slots), 1)
            for i in range(TOGETHER):
                r = index * TOGETHER + i
                queries = query_heads[r]
                scores = lax.dot_general(
                    queries.astype(BF16),
                    keys[r],
                    (((1,), (1,)), ((), ())),
                    preferred_element_type=F32,
                )
                scores = jnp.where(place < lengths_ref[r], scores * score_scale, -1e30)
                fresh = jnp.sum(queries * fresh_keys[pl.ds(r, 1)], -1, keepdims=True)
                fresh = fresh * score_scale
                highest = jnp.maximum(jnp.max(scores, -1, keepdims=True), fresh)
                weights = jnp.exp(scores - highest)
                own = jnp.exp(fresh - highest)
                total = jnp.sum(weights, -1, keepdims=True) + own
                mixed = jnp.dot(weights.astype(BF16), values[r], preferred_element_type=F32)
                mixed = mixed + own * fresh_values[pl.ds(r, 1)]
                mixed_heads[r] = mixed / total
            return carry

        lax.fori_loop(a * blocks, (a + 1) * blocks, requests, 0)
        place = slice(a * half, (a + 1) * half)
        for i in range(heads):
            attn[a, :, i * head_size : (i + 1) * head_size] = mixed_heads[place, i, :].astype(BF16)

    parts, shared, gathers, pairs, swaps, planes, lasts = {}, {}, {}, {}, {}, {}, {}

    def project_out(a):
        for k in order:
            if a == 0:
                loads["proj", k].wait()
            term = jnp.dot(attn[a], proj[k], preferred_element_type=F32)
            if k:
                part_send[a, k] = term.astype(BF16)
                parts[a, k] = send(
                    part_send.at[a, k], part_recv.at[a, k], part_sems, (a, k), above[k]
                )
            else:
                own = pl.ds(pl.multiple_of(head * share, share), share)
                hidden[a] = term + x_ref[a * half : (a + 1) * half, own].astype(F32)

    def share_hidden(a):
        total = hidden[a]
        for k in order[:-1]:
            parts[a, k].wait_recv()
            total = total + part_recv[a, k].astype(F32)
        hidden[a] = total
        slabs[a, 0] = total.astype(BF16)
        for k in order[:-1]:
            shared[a, k] = send(slabs.at[a, 0], slabs.at[a, k], slab_sems, (a, k), above[k])

    def gate_table(a):
        place = slice(a * half, (a + 1) * half)
        lane = lax.broadcasted_iota(jnp.int32, (half, lanes), 1)
        expert = jnp.where(lane < experts, lane, lane - experts)
        ids, weights = ids_ref[place, :], gate_weight_ref[place, :]
        table = jnp.zeros((half, lanes), F32)
        for i in range(ids.shape[1]):
            table += jnp.where(ids[:, i : i + 1] == expert, weights[:, i : i + 1], 0.0)
        first = table.astype(BF16).astype(F32)
        return jnp.where(lane < experts, first, table - first).astype(BF16)

    def norm_and_gather(a):
        rows_all[a, 0, :, width:] = gate_table(a)
        for k in order[:-1]:
            shared[a, k].wait_recv()
        squares = jnp.zeros((half, 1), F32)
        for k in range(groups):
            value = slabs[a, k].astype(F32)
            squares = squares + jnp.sum(value * value, -1, keepdims=True)
        scale = lax.rsqrt(squares / width + 1e-06)
        for k in range(groups):
            slab_gain = gain_ref[(head - k + groups) % groups]
            rows_all[a, 0, :, k * share : (k + 1) * share] = (
                slabs[a, k].astype(F32) * scale * slab_gain
            ).astype(BF16)
        for q in range(1, chips):
            gathers[a, q] = send(
                rows_all.at[a, 0], rows_all.at[a, q], gather_sems, (a, q), across[q]
            )
        pairs[a, 0] = send(
            rows_all.at[a, 0], rows_all.at[a, chips], pair_sems, (a, 0), partner
        )

    def pass_to_partner(a):
        for q in range(1, chips):
            gathers[a, q].wait_recv()
            pairs[a, q] = send(
                rows_all.at[a, q], rows_all.at[a, chips + q], pair_sems, (a, q), partner
            )
        for q in range(chips):
            pairs[a, q].wait_recv()

    block = min(16, pools)

    def expert_rows(a):
        if a == 0:
            for k in range(groups):
                for e in range(local):
                    loads["gate", (e, k)].wait()
                    loads["up", (e, k)].wait()

        def some_rows(index, carry):
            place = pl.ds(index * block, block)
            gates = rows_all[a, place, :, width:].reshape(block * half, -1).astype(F32)
            lane = lax.broadcasted_iota(jnp.int32, gates.shape, 1)
            for e in range(local):
                gate_part = jnp.zeros((block * half, units), F32)
                up_part = jnp.zeros((block * half, units), F32)
                for k in range(groups):
                    piece = rows_all[a, place, :, k * share : (k + 1) * share].reshape(
                        block * half, share
                    )
                    gate_part += jnp.dot(piece, gate[e, k], preferred_element_type=F32)
                    up_part += jnp.dot(piece, up[e, k], preferred_element_type=F32)
                expert = pool * local + e
                chosen = (lane == expert) | (lane == experts + expert)
                weight = jnp.sum(jnp.where(chosen, gates, 0.0), -1, keepdims=True)
                value = gate_part / (1.0 + jnp.exp(-gate_part)) * up_part * weight
                act[place, :, e * units : (e + 1) * units] = value.astype(BF16).reshape(
                    block, half, units
                )
            return carry

        lax.fori_loop(0, pools // block, some_rows, 0)

    def project_down(a, k):
        if a == 0:
            for e in range(local):
                loads["down", (e, k)].wait()

        def some_rows(index, carry):
            place = pl.ds(index * block, block)
            value = jnp.dot(
                act[place].reshape(block * half, local * units),
                down[k].reshape(local * units, share),
                preferred_element_type=F32,
            )
            produced[a, k, place] = value.astype(BF16).reshape(block, half, share)
            return carry

        lax.fori_loop(0, pools // block, some_rows, 0)
        swaps[a, k] = send(
            produced.at[a, k, pl.ds(chips, chips)],
            pair_recv.at[a, k],
            swap_sems,
            (a, k),
            partner,
        )

    def cross(a, k):
        swaps[a, k].wait_recv()
        for q in range(1, chips):
            produced[a, k, q] = (
                produced[a, k, q].astype(F32) + pair_recv[a, k, q].astype(F32)
            ).astype(BF16)
            planes[a, k, q] = send(
                produced.at[a, k, q],
                plane_recv.at[a, k, q],
                plane_sems,
                (a, k, q),
                across[q],
            )

    def finish(a, k):
        value = produced[a, k, 0].astype(F32) + pair_recv[a, k, 0].astype(F32)
        for q in range(1, chips):
            planes[a, k, q].wait_recv()
            value = value + plane_recv[a, k, q].astype(F32)
        if k:
            last_send[a, k] = value.astype(BF16)
            lasts[a, k] = send(
                last_send.at[a, k], last_recv.at[a, k], last_sems, (a, k), above[k]
            )
        else:
            hidden[a] = hidden[a] + value

    def write(a):
        value = hidden[a]
        for k in order[:-1]:
            lasts[a, k].wait_recv()
            value = value + last_recv[a, k].astype(F32)
        out_ref[a * half : (a + 1) * half, :] = value

    def experts_out(a, between):
        expert_rows(a)
        for step in range(groups + 1):
            if step < groups:
                project_down(a, order[step])
            if step:
                cross(a, order[step - 1])
                between(order[step - 1])

    attend(0)
    pl.semaphore_wait(barrier, len(greeted))
    project_out(0)
    attend(1)
    share_hidden(0)
    project_out(1)
    norm_and_gather(0)
    share_hidden(1)
    norm_and_gather(1)
    pass_to_partner(0)
    experts_out(0, lambda k: None)
    pass_to_partner(1)
    experts_out(1, lambda k: finish(0, k))
    for k in order:
        finish(1, k)
    write(0)
    write(1)
    for copy in sent:
        copy.wait_send()


def body(
    x_rows,
    query,
    key_cache,
    value_cache,
    new_key,
    new_value,
    lengths,
    out_proj,
    norm_gain,
    expert_ids,
    gate_weights,
    w_gate,
    w_up,
    w_down,
):
    pools = lax.axis_size("pool")
    groups = lax.axis_size("head")
    rows, width = x_rows.shape
    share = width // groups
    local, _, units = w_gate.shape
    experts = pools * local
    chips = pools // 2
    half = rows // HALVES
    head_size = new_key.shape[1]
    heads = query.shape[1] // head_size
    slots = key_cache.shape[2]
    lanes = -(-2 * experts // 128) * 128
    depth = out_proj.shape[0]
    in_smem = pl.BlockSpec(memory_space=pltpu.SMEM)
    in_vmem = pl.BlockSpec(memory_space=pltpu.VMEM)
    in_hbm = pl.BlockSpec(memory_space=pl.ANY)
    dma = pltpu.SemaphoreType.DMA
    summed = pl.pallas_call(
        functools.partial(layer_kernel, pools, groups, experts),
        out_shape=jax.ShapeDtypeStruct((rows, share), F32),
        in_specs=[in_smem] + [in_vmem] * 7 + [in_hbm] * 6,
        out_specs=in_vmem,
        scratch_shapes=[
            pltpu.VMEM((rows, slots, head_size), BF16),
            pltpu.VMEM((rows, slots, head_size), BF16),
            pltpu.VMEM((rows, heads, head_size), F32),
            pltpu.VMEM((rows, heads, head_size), F32),
            pltpu.VMEM((rows, head_size), F32),
            pltpu.VMEM((rows, head_size), F32),
            pltpu.VMEM((HALVES, half, depth), BF16),
            pltpu.VMEM((groups, depth, share), BF16),
            pltpu.VMEM((local, groups, share, units), BF16),
            pltpu.VMEM((local, groups, share, units), BF16),
            pltpu.VMEM((groups, local, units, share), BF16),
            pltpu.VMEM((HALVES, groups, half, share), BF16),
            pltpu.VMEM((HALVES, groups, half, share), BF16),
            pltpu.VMEM((HALVES, half, share), F32),
            pltpu.VMEM((HALVES, groups, half, share), BF16),
            pltpu.VMEM((HALVES, pools, half, width + lanes), BF16),
            pltpu.VMEM((pools, half, local * units), BF16),
            pltpu.VMEM((HALVES, groups, pools, half, share), BF16),
            pltpu.VMEM((HALVES, groups, chips, half, share), BF16),
            pltpu.VMEM((HALVES, groups, chips, half, share), BF16),
            pltpu.VMEM((HALVES, groups, half, share), BF16),
            pltpu.VMEM((HALVES, groups, half, share), BF16),
            dma((2, rows // TOGETHER)),
            dma((groups * (1 + 3 * local),)),
            dma((2, HALVES, groups)),
            dma((2, HALVES, groups)),
            dma((2, HALVES, chips)),
            dma((2, HALVES, chips)),
            dma((2, HALVES, groups)),
            dma((2, HALVES, groups, chips)),
            dma((2, HALVES, groups)),
        ],
        compiler_params=pltpu.CompilerParams(
            collective_id=0, has_side_effects=True, vmem_limit_bytes=VMEM_BYTES
        ),
    )(
        lengths,
        query,
        new_key,
        new_value,
        x_rows,
        expert_ids,
        gate_weights,
        norm_gain.reshape(groups, 1, share),
        key_cache,
        value_cache,
        out_proj,
        w_gate,
        w_up,
        w_down,
    )
    return summed.astype(BF16)


def solution(mesh):
    placed = (
        P("pool", None),
        P("pool", "head"),
        P("pool", "head", None, None),
        P("pool", "head", None, None),
        P("pool", "head"),
        P("pool", "head"),
        P("pool"),
        P("head", None),
        P(),
        P("pool", None),
        P("pool", None),
        P("pool", None, "head"),
        P("pool", None, "head"),
        P("pool", "head", None),
    )
    return jax.shard_map(
        body, mesh=mesh, in_specs=placed, out_specs=P("pool", "head"), check_vma=False
    )
```

```python
import functools

import jax
import jax.numpy as jnp
from jax import lax
from jax.experimental import pallas as pl
from jax.experimental.pallas import tpu as pltpu
from jax.sharding import PartitionSpec as P

VMEM_BYTES = 60 * 1024 * 1024
HALVES = 2
TOGETHER = 8

MESH = pl.DeviceIdType.MESH
F32 = jnp.float32
BF16 = jnp.bfloat16


def flip(index, offset, count):
    result, bit = 0, 1
    while bit < count:
        result = result + bit * ((index // bit + offset // bit) % 2)
        bit *= 2
    return result


def layer_kernel(
    pools,
    groups,
    experts,
    lengths_ref,
    query_ref,
    new_key_ref,
    new_value_ref,
    x_ref,
    ids_ref,
    gate_weight_ref,
    gain_ref,
    key_hbm,
    value_hbm,
    proj_hbm,
    gate_hbm,
    up_hbm,
    down_hbm,
    out_ref,
    keys,
    values,
    query_heads,
    mixed_heads,
    fresh_keys,
    fresh_values,
    attn,
    proj,
    gate,
    up,
    down,
    part_send,
    part_recv,
    hidden,
    slabs,
    rows_all,
    act,
    produced,
    pair_recv,
    plane_recv,
    first_send,
    first_recv,
    second_send,
    second_recv,
    last_send,
    last_recv,
    cache_sem,
    load_sem,
    part_sems,
    slab_sems,
    gather_sems,
    pair_sems,
    swap_sems,
    plane_sems,
    last_sems,
):
    chips = pools // 2
    half, share = hidden.shape[1:]
    width = groups * share
    local = gate.shape[0]
    units = gate.shape[3]
    lanes = rows_all.shape[3] - width
    heads, head_size = query_heads.shape[1:]
    slots = keys.shape[1]
    pool, head = lax.axis_index("pool"), lax.axis_index("head")
    chip, core = pool // 2, pool % 2
    partner = {"pool": chip * 2 + 1 - core}
    above = [{"head": (head + k) % groups} for k in range(groups)]
    across = [{"pool": flip(chip, q, chips) * 2 + core} for q in range(chips)]
    order = list(range(1, groups)) + [0]
    sent = []
    relayed = chips == 4
    cuts = [pl.ds(0, width // 2), pl.ds(width // 2, width - width // 2 + lanes)]
    sides = [slice(0, share // 2), slice(share // 2, share)]

    def send(source, target, sems, place, device):
        copy = pltpu.make_async_remote_copy(
            src_ref=source,
            dst_ref=target,
            send_sem=sems.at[(0,) + place],
            recv_sem=sems.at[(1,) + place],
            device_id=device,
            device_id_type=MESH,
        )
        copy.start()
        sent.append(copy)
        return copy

    loads = {}

    def load(name, index, source, target):
        copy = pltpu.make_async_copy(source, target, load_sem.at[len(loads)])
        copy.start()
        loads[name, index] = copy

    def columns(k):
        return pl.ds(pl.multiple_of((head + k) % groups * share, share), share)

    def depths(k):
        return pl.ds(pl.multiple_of((head - k + groups) % groups * share, share), share)

    def cache_copies(index):
        place = pl.ds(index * TOGETHER, TOGETHER)
        return [
            pltpu.make_async_copy(key_hbm.at[place, 0], keys.at[place], cache_sem.at[0, index]),
            pltpu.make_async_copy(
                value_hbm.at[place, 0], values.at[place], cache_sem.at[1, index]
            ),
        ]

    blocks = half // TOGETHER

    def load_cache(a):
        for index in range(a * blocks, (a + 1) * blocks):
            for copy in cache_copies(index):
                copy.start()

    load_cache(0)
    for k in order:
        load("proj", k, proj_hbm.at[:, columns(k)], proj.at[k])
    for a in range(1, HALVES):
        load_cache(a)
    for k in range(groups):
        for e in range(local):
            load("gate", (e, k), gate_hbm.at[e, depths(k)], gate.at[e, k])
            load("up", (e, k), up_hbm.at[e, depths(k)], up.at[e, k])
    for k in order:
        for e in range(local):
            load("down", (e, k), down_hbm.at[e, :, columns(k)], down.at[k, e])

    barrier = pltpu.get_barrier_semaphore()
    greeted = above[1:] + across[1:] + [partner]
    for device in greeted:
        pl.semaphore_signal(barrier, inc=1, device_id=device, device_id_type=MESH)

    for i in range(heads):
        query_heads[:, i, :] = query_ref[:, i * head_size : (i + 1) * head_size].astype(F32)
    fresh_keys[...] = new_key_ref[...].astype(F32)
    fresh_values[...] = new_value_ref[...].astype(F32)
    score_scale = head_size ** (-0.5)

    rows = HALVES * half
    lane = lax.broadcasted_iota(jnp.int32, (lanes, rows), 0)
    named = jnp.where(lane < experts, lane, lane - experts)
    table = jnp.zeros((lanes, rows), F32)
    for i in range(ids_ref.shape[0]):
        table += jnp.where(ids_ref[i : i + 1, :] == named, gate_weight_ref[i : i + 1, :], 0.0)
    first = table.astype(BF16).astype(F32)
    terms = jnp.where(lane < experts, first, table - first).astype(BF16)
    square = (rows, rows)
    eye = lax.broadcasted_iota(jnp.int32, square, 0) == lax.broadcasted_iota(jnp.int32, square, 1)
    terms = lax.dot_general(
        eye.astype(F32).astype(BF16), terms, (((1,), (1,)), ((), ())), preferred_element_type=F32
    ).astype(BF16)
    for a in range(HALVES):
        rows_all[a, 0, :, width:] = terms[a * half : (a + 1) * half]

    def attend(a):
        def requests(index, carry):
            for copy in cache_copies(index):
                copy.wait()
            place = lax.broadcasted_iota(jnp.int32, (heads, slots), 1)
            for i in range(TOGETHER):
                r = index * TOGETHER + i
                queries = query_heads[r]
                scores = lax.dot_general(
                    queries.astype(BF16),
                    keys[r],
                    (((1,), (1,)), ((), ())),
                    preferred_element_type=F32,
                )
                scores = jnp.where(place < lengths_ref[r], scores * score_scale, -1e30)
                fresh = jnp.sum(queries * fresh_keys[pl.ds(r, 1)], -1, keepdims=True)
                fresh = fresh * score_scale
                highest = jnp.maximum(jnp.max(scores, -1, keepdims=True), fresh)
                weights = jnp.exp(scores - highest)
                own = jnp.exp(fresh - highest)
                total = jnp.sum(weights, -1, keepdims=True) + own
                mixed = jnp.dot(weights.astype(BF16), values[r], preferred_element_type=F32)
                mixed = mixed + own * fresh_values[pl.ds(r, 1)]
                mixed_heads[r] = mixed / total
            return carry

        lax.fori_loop(a * blocks, (a + 1) * blocks, requests, 0)
        place = slice(a * half, (a + 1) * half)
        for i in range(heads):
            attn[a, :, i * head_size : (i + 1) * head_size] = mixed_heads[place, i, :].astype(BF16)

    parts, shared, gathers, pairs, swaps, planes, lasts = {}, {}, {}, {}, {}, {}, {}

    def project_out(a):
        for k in order:
            if a == 0:
                loads["proj", k].wait()
            term = jnp.dot(attn[a], proj[k], preferred_element_type=F32)
            if k:
                part_send[a, k] = term.astype(BF16)
                parts[a, k] = send(
                    part_send.at[a, k], part_recv.at[a, k], part_sems, (a, k), above[k]
                )
            else:
                own = pl.ds(pl.multiple_of(head * share, share), share)
                hidden[a] = term + x_ref[a * half : (a + 1) * half, own].astype(F32)

    def share_hidden(a):
        total = hidden[a]
        for k in order[:-1]:
            parts[a, k].wait_recv()
            total = total + part_recv[a, k].astype(F32)
        hidden[a] = total
        slabs[a, 0] = total.astype(BF16)
        for k in order[:-1]:
            shared[a, k] = send(slabs.at[a, 0], slabs.at[a, k], slab_sems, (a, k), above[k])

    def norm_and_gather(a):
        for k in order[:-1]:
            shared[a, k].wait_recv()
        squares = jnp.zeros((half, 1), F32)
        for k in range(groups):
            value = slabs[a, k].astype(F32)
            squares = squares + jnp.sum(value * value, -1, keepdims=True)
        scale = lax.rsqrt(squares / width + 1e-06)
        for k in range(groups):
            slab_gain = gain_ref[(head - k + groups) % groups]
            rows_all[a, 0, :, k * share : (k + 1) * share] = (
                slabs[a, k].astype(F32) * scale * slab_gain
            ).astype(BF16)
        pairs[a, 0] = send(
            rows_all.at[a, 0], rows_all.at[a, chips], pair_sems, (a, 0), partner
        )
        if relayed:
            for q, c in ((1, 0), (2, 1), (1, 1), (2, 0)):
                gathers[a, q, c] = send(
                    rows_all.at[a, 0, :, cuts[c]],
                    rows_all.at[a, q, :, cuts[c]],
                    gather_sems,
                    (a, q, c),
                    across[q],
                )
        else:
            for q in range(1, chips):
                gathers[a, q] = send(
                    rows_all.at[a, 0], rows_all.at[a, q], gather_sems, (a, q, 0), across[q]
                )

    def relay(a):
        if relayed:
            for c, near, far in ((0, 1, 2), (1, 2, 1)):
                gathers[a, near, c].wait_recv()
                gathers[a, 3, c] = send(
                    rows_all.at[a, near, :, cuts[c]],
                    rows_all.at[a, 3, :, cuts[c]],
                    gather_sems,
                    (a, 3, c),
                    across[far],
                )

    def pass_to_partner(a):
        for q in range(1, chips):
            if not relayed:
                gathers[a, q].wait_recv()
            elif q < 3:
                gathers[a, q, 2 - q].wait_recv()
            else:
                gathers[a, q, 0].wait_recv()
                gathers[a, q, 1].wait_recv()
            pairs[a, q] = send(
                rows_all.at[a, q], rows_all.at[a, chips + q], pair_sems, (a, q), partner
            )
        for q in range(chips):
            pairs[a, q].wait_recv()

    block = min(16, pools)

    def expert_rows(a):
        if a == 0:
            for k in range(groups):
                for e in range(local):
                    loads["gate", (e, k)].wait()
                    loads["up", (e, k)].wait()

        def some_rows(index, carry):
            place = pl.ds(index * block, block)
            gates = rows_all[a, place, :, width:].reshape(block * half, -1).astype(F32)
            lane = lax.broadcasted_iota(jnp.int32, gates.shape, 1)
            for e in range(local):
                gate_part = jnp.zeros((block * half, units), F32)
                up_part = jnp.zeros((block * half, units), F32)
                for k in range(groups):
                    piece = rows_all[a, place, :, k * share : (k + 1) * share].reshape(
                        block * half, share
                    )
                    gate_part += jnp.dot(piece, gate[e, k], preferred_element_type=F32)
                    up_part += jnp.dot(piece, up[e, k], preferred_element_type=F32)
                expert = pool * local + e
                chosen = (lane == expert) | (lane == experts + expert)
                weight = jnp.sum(jnp.where(chosen, gates, 0.0), -1, keepdims=True)
                value = gate_part / (1.0 + jnp.exp(-gate_part)) * up_part * weight
                act[place, :, e * units : (e + 1) * units] = value.astype(BF16).reshape(
                    block, half, units
                )
            return carry

        lax.fori_loop(0, pools // block, some_rows, 0)

    def project_down(a, k):
        if a == 0:
            for e in range(local):
                loads["down", (e, k)].wait()

        def some_rows(index, carry):
            place = pl.ds(index * block, block)
            value = jnp.dot(
                act[place].reshape(block * half, local * units),
                down[k].reshape(local * units, share),
                preferred_element_type=F32,
            )
            produced[a, k, place] = value.astype(BF16).reshape(block, half, share)
            return carry

        lax.fori_loop(0, pools // block, some_rows, 0)
        swaps[a, k] = send(
            produced.at[a, k, pl.ds(chips, chips)],
            pair_recv.at[a, k],
            swap_sems,
            (a, k),
            partner,
        )

    def summed(a, k, q, side=slice(None)):
        return produced[a, k, q, :, side].astype(F32) + pair_recv[a, k, q, :, side].astype(F32)

    def cross(a, k):
        swaps[a, k].wait_recv()
        if relayed:
            for d in range(2):
                first_send[a, k, d, 0] = summed(a, k, 1 + d, sides[d]).astype(BF16)
                first_send[a, k, d, 1] = summed(a, k, 3, sides[d]).astype(BF16)
                planes[a, k, d] = send(
                    first_send.at[a, k, d],
                    first_recv.at[a, k, d],
                    plane_sems,
                    (a, k, d),
                    across[1 + d],
                )
        else:
            for q in range(1, chips):
                produced[a, k, q] = summed(a, k, q).astype(BF16)
                planes[a, k, q] = send(
                    produced.at[a, k, q],
                    plane_recv.at[a, k, q],
                    plane_sems,
                    (a, k, q),
                    across[q],
                )

    def cross_again(a, k):
        if relayed:
            for d in range(2):
                planes[a, k, d].wait_recv()
                value = summed(a, k, 2 - d, sides[d]) + first_recv[a, k, d, 1].astype(F32)
                second_send[a, k, d] = value.astype(BF16)
                planes[a, k, 2 + d] = send(
                    second_send.at[a, k, d],
                    second_recv.at[a, k, d],
                    plane_sems,
                    (a, k, 2 + d),
                    across[2 - d],
                )

    def finish(a, k):
        value = summed(a, k, 0)
        if relayed:
            planes[a, k, 2].wait_recv()
            planes[a, k, 3].wait_recv()
            came = [
                first_recv[a, k, d, 0].astype(F32) + second_recv[a, k, d].astype(F32)
                for d in range(2)
            ]
            value = value + jnp.concatenate(came, 1)
        else:
            for q in range(1, chips):
                planes[a, k, q].wait_recv()
                value = value + plane_recv[a, k, q].astype(F32)
        if k:
            last_send[a, k] = value.astype(BF16)
            lasts[a, k] = send(
                last_send.at[a, k], last_recv.at[a, k], last_sems, (a, k), above[k]
            )
        else:
            hidden[a] = hidden[a] + value

    def write(a):
        value = hidden[a]
        for k in order[:-1]:
            lasts[a, k].wait_recv()
            value = value + last_recv[a, k].astype(F32)
        out_ref[a * half : (a + 1) * half, :] = value

    def down_out(a, between):
        for step in range(groups + 2):
            if step < groups:
                project_down(a, order[step])
            if 1 <= step <= groups:
                cross(a, order[step - 1])
                between(order[step - 1])
            if step >= 2:
                cross_again(a, order[step - 2])

    attend(0)
    pl.semaphore_wait(barrier, len(greeted))
    project_out(0)
    attend(1)
    share_hidden(0)
    project_out(1)
    norm_and_gather(0)
    share_hidden(1)
    relay(0)
    norm_and_gather(1)
    pass_to_partner(0)
    expert_rows(0)
    relay(1)
    down_out(0, lambda k: None)
    pass_to_partner(1)
    expert_rows(1)
    down_out(1, lambda k: finish(0, k))
    for k in order:
        finish(1, k)
    write(0)
    write(1)
    for copy in sent:
        copy.wait_send()


def body(
    x_rows,
    query,
    key_cache,
    value_cache,
    new_key,
    new_value,
    lengths,
    out_proj,
    norm_gain,
    expert_ids,
    gate_weights,
    w_gate,
    w_up,
    w_down,
):
    pools = lax.axis_size("pool")
    groups = lax.axis_size("head")
    rows, width = x_rows.shape
    share = width // groups
    local, _, units = w_gate.shape
    experts = pools * local
    chips = pools // 2
    half = rows // HALVES
    head_size = new_key.shape[1]
    heads = query.shape[1] // head_size
    slots = key_cache.shape[2]
    lanes = -(-2 * experts // 128) * 128
    depth = out_proj.shape[0]
    relayed = chips == 4
    first = (HALVES, groups, 2, 2, half, share // 2) if relayed else (1,) * 6
    second = (HALVES, groups, 2, half, share // 2) if relayed else (1,) * 5
    in_smem = pl.BlockSpec(memory_space=pltpu.SMEM)
    in_vmem = pl.BlockSpec(memory_space=pltpu.VMEM)
    in_hbm = pl.BlockSpec(memory_space=pl.ANY)
    dma = pltpu.SemaphoreType.DMA
    summed = pl.pallas_call(
        functools.partial(layer_kernel, pools, groups, experts),
        out_shape=jax.ShapeDtypeStruct((rows, share), F32),
        in_specs=[in_smem] + [in_vmem] * 7 + [in_hbm] * 6,
        out_specs=in_vmem,
        scratch_shapes=[
            pltpu.VMEM((rows, slots, head_size), BF16),
            pltpu.VMEM((rows, slots, head_size), BF16),
            pltpu.VMEM((rows, heads, head_size), F32),
            pltpu.VMEM((rows, heads, head_size), F32),
            pltpu.VMEM((rows, head_size), F32),
            pltpu.VMEM((rows, head_size), F32),
            pltpu.VMEM((HALVES, half, depth), BF16),
            pltpu.VMEM((groups, depth, share), BF16),
            pltpu.VMEM((local, groups, share, units), BF16),
            pltpu.VMEM((local, groups, share, units), BF16),
            pltpu.VMEM((groups, local, units, share), BF16),
            pltpu.VMEM((HALVES, groups, half, share), BF16),
            pltpu.VMEM((HALVES, groups, half, share), BF16),
            pltpu.VMEM((HALVES, half, share), F32),
            pltpu.VMEM((HALVES, groups, half, share), BF16),
            pltpu.VMEM((HALVES, pools, half, width + lanes), BF16),
            pltpu.VMEM((pools, half, local * units), BF16),
            pltpu.VMEM((HALVES, groups, pools, half, share), BF16),
            pltpu.VMEM((HALVES, groups, chips, half, share), BF16),
            pltpu.VMEM((1,) * 5 if relayed else (HALVES, groups, chips, half, share), BF16),
            pltpu.VMEM(first, BF16),
            pltpu.VMEM(first, BF16),
            pltpu.VMEM(second, BF16),
            pltpu.VMEM(second, BF16),
            pltpu.VMEM((HALVES, groups, half, share), BF16),
            pltpu.VMEM((HALVES, groups, half, share), BF16),
            dma((2, rows // TOGETHER)),
            dma((groups * (1 + 3 * local),)),
            dma((2, HALVES, groups)),
            dma((2, HALVES, groups)),
            dma((2, HALVES, chips, 2)),
            dma((2, HALVES, chips)),
            dma((2, HALVES, groups)),
            dma((2, HALVES, groups, chips)),
            dma((2, HALVES, groups)),
        ],
        compiler_params=pltpu.CompilerParams(
            collective_id=0, has_side_effects=True, vmem_limit_bytes=VMEM_BYTES
        ),
    )(
        lengths,
        query,
        new_key,
        new_value,
        x_rows,
        expert_ids.T,
        gate_weights.T,
        norm_gain.reshape(groups, 1, share),
        key_cache,
        value_cache,
        out_proj,
        w_gate,
        w_up,
        w_down,
    )
    return summed.astype(BF16)


def solution(mesh):
    placed = (
        P("pool", None),
        P("pool", "head"),
        P("pool", "head", None, None),
        P("pool", "head", None, None),
        P("pool", "head"),
        P("pool", "head"),
        P("pool"),
        P("head", None),
        P(),
        P("pool", None),
        P("pool", None),
        P("pool", None, "head"),
        P("pool", None, "head"),
        P("pool", "head", None),
    )
    return jax.shard_map(
        body, mesh=mesh, in_specs=placed, out_specs=P("pool", "head"), check_vma=False
    )
```

```python
import functools

import jax
import jax.numpy as jnp
from jax import lax
from jax.experimental import pallas as pl
from jax.experimental.pallas import tpu as pltpu
from jax.sharding import PartitionSpec as P

VMEM_BYTES = 60 * 1024 * 1024
HALVES = 2
TOGETHER = 8

MESH = pl.DeviceIdType.MESH
F32 = jnp.float32
BF16 = jnp.bfloat16


def flip(index, offset, count):
    result, bit = 0, 1
    while bit < count:
        result = result + bit * ((index // bit + offset // bit) % 2)
        bit *= 2
    return result


def layer_kernel(
    pools,
    groups,
    experts,
    lengths_ref,
    query_ref,
    new_key_ref,
    new_value_ref,
    x_ref,
    ids_ref,
    gate_weight_ref,
    gain_ref,
    key_hbm,
    value_hbm,
    proj_hbm,
    gate_hbm,
    up_hbm,
    down_hbm,
    out_ref,
    keys,
    values,
    query_heads,
    mixed_heads,
    fresh_keys,
    fresh_values,
    attn,
    proj,
    gate,
    up,
    down,
    part_send,
    part_recv,
    hidden,
    slabs,
    rows_all,
    act,
    produced,
    pair_recv,
    plane_recv,
    last_send,
    last_recv,
    cache_sem,
    load_sem,
    part_sems,
    slab_sems,
    gather_sems,
    pair_sems,
    swap_sems,
    plane_sems,
    last_sems,
):
    chips = pools // 2
    half, share = hidden.shape[1:]
    width = groups * share
    local = gate.shape[0]
    units = gate.shape[3]
    lanes = rows_all.shape[3] - width
    heads, head_size = query_heads.shape[1:]
    slots = keys.shape[1]
    pool, head = lax.axis_index("pool"), lax.axis_index("head")
    chip, core = pool // 2, pool % 2
    partner = {"pool": chip * 2 + 1 - core}
    above = [{"head": (head + k) % groups} for k in range(groups)]
    across = [{"pool": flip(chip, q, chips) * 2 + core} for q in range(chips)]
    order = list(range(1, groups)) + [0]
    sent = []

    def send(source, target, sems, place, device):
        copy = pltpu.make_async_remote_copy(
            src_ref=source,
            dst_ref=target,
            send_sem=sems.at[(0,) + place],
            recv_sem=sems.at[(1,) + place],
            device_id=device,
            device_id_type=MESH,
        )
        copy.start()
        sent.append(copy)
        return copy

    loads = {}

    def load(name, index, source, target):
        copy = pltpu.make_async_copy(source, target, load_sem.at[len(loads)])
        copy.start()
        loads[name, index] = copy

    def columns(k):
        return pl.ds(pl.multiple_of((head + k) % groups * share, share), share)

    def depths(k):
        return pl.ds(pl.multiple_of((head - k + groups) % groups * share, share), share)

    def cache_copies(index):
        place = pl.ds(index * TOGETHER, TOGETHER)
        return [
            pltpu.make_async_copy(key_hbm.at[place, 0], keys.at[place], cache_sem.at[0, index]),
            pltpu.make_async_copy(
                value_hbm.at[place, 0], values.at[place], cache_sem.at[1, index]
            ),
        ]

    blocks = half // TOGETHER

    def load_cache(a):
        for index in range(a * blocks, (a + 1) * blocks):
            for copy in cache_copies(index):
                copy.start()

    load_cache(0)
    for k in order:
        load("proj", k, proj_hbm.at[:, columns(k)], proj.at[k])
    for a in range(1, HALVES):
        load_cache(a)
    for k in range(groups):
        for e in range(local):
            load("gate", (e, k), gate_hbm.at[e, depths(k)], gate.at[e, k])
            load("up", (e, k), up_hbm.at[e, depths(k)], up.at[e, k])
    for k in order:
        for e in range(local):
            load("down", (e, k), down_hbm.at[e, :, columns(k)], down.at[k, e])

    barrier = pltpu.get_barrier_semaphore()
    greeted = above[1:] + across[1:] + [partner]
    for device in greeted:
        pl.semaphore_signal(barrier, inc=1, device_id=device, device_id_type=MESH)

    for i in range(heads):
        query_heads[:, i, :] = query_ref[:, i * head_size : (i + 1) * head_size].astype(F32)
    fresh_keys[...] = new_key_ref[...].astype(F32)
    fresh_values[...] = new_value_ref[...].astype(F32)
    score_scale = head_size ** (-0.5)

    rows = HALVES * half
    lane = lax.broadcasted_iota(jnp.int32, (lanes, rows), 0)
    named = jnp.where(lane < experts, lane, lane - experts)
    table = jnp.zeros((lanes, rows), F32)
    for i in range(ids_ref.shape[0]):
        table += jnp.where(ids_ref[i : i + 1, :] == named, gate_weight_ref[i : i + 1, :], 0.0)
    first = table.astype(BF16).astype(F32)
    terms = jnp.where(lane < experts, first, table - first).astype(BF16)
    square = (rows, rows)
    eye = lax.broadcasted_iota(jnp.int32, square, 0) == lax.broadcasted_iota(jnp.int32, square, 1)
    terms = lax.dot_general(
        eye.astype(F32).astype(BF16), terms, (((1,), (1,)), ((), ())), preferred_element_type=F32
    ).astype(BF16)
    for a in range(HALVES):
        rows_all[a, 0, :, width:] = terms[a * half : (a + 1) * half]

    def attend(a):
        def requests(index, carry):
            for copy in cache_copies(index):
                copy.wait()
            place = lax.broadcasted_iota(jnp.int32, (heads, slots), 1)
            numbers = [index * TOGETHER + i for i in range(TOGETHER)]
            queries = [query_heads[r] for r in numbers]
            scores = [
                lax.dot_general(
                    query.astype(BF16),
                    keys[r],
                    (((1,), (1,)), ((), ())),
                    preferred_element_type=F32,
                )
                for r, query in zip(numbers, queries)
            ]
            scores = [
                jnp.where(place < lengths_ref[r], score * score_scale, -1e30)
                for r, score in zip(numbers, scores)
            ]
            fresh = [
                jnp.sum(query * fresh_keys[pl.ds(r, 1)], -1, keepdims=True) * score_scale
                for r, query in zip(numbers, queries)
            ]
            highest = [
                jnp.maximum(jnp.max(score, -1, keepdims=True), new)
                for score, new in zip(scores, fresh)
            ]
            weights = [jnp.exp(score - top) for score, top in zip(scores, highest)]
            mixed = [
                jnp.dot(weight.astype(BF16), values[r], preferred_element_type=F32)
                for r, weight in zip(numbers, weights)
            ]
            own = [jnp.exp(new - top) for new, top in zip(fresh, highest)]
            totals = [
                jnp.sum(weight, -1, keepdims=True) + new for weight, new in zip(weights, own)
            ]
            mixed = [
                (value + new * fresh_values[pl.ds(r, 1)]) / total
                for r, value, new, total in zip(numbers, mixed, own, totals)
            ]
            for r, value in zip(numbers, mixed):
                mixed_heads[r] = value
            return carry

        lax.fori_loop(a * blocks, (a + 1) * blocks, requests, 0)
        place = slice(a * half, (a + 1) * half)
        for i in range(heads):
            attn[a, :, i * head_size : (i + 1) * head_size] = mixed_heads[place, i, :].astype(BF16)

    parts, shared, gathers, pairs, swaps, planes, lasts = {}, {}, {}, {}, {}, {}, {}

    def project_out(a):
        for k in order:
            if a == 0:
                loads["proj", k].wait()
            term = jnp.dot(attn[a], proj[k], preferred_element_type=F32)
            if k:
                part_send[a, k] = term.astype(BF16)
                parts[a, k] = send(
                    part_send.at[a, k], part_recv.at[a, k], part_sems, (a, k), above[k]
                )
            else:
                own = pl.ds(pl.multiple_of(head * share, share), share)
                hidden[a] = term + x_ref[a * half : (a + 1) * half, own].astype(F32)

    def share_hidden(a):
        total = hidden[a]
        for k in order[:-1]:
            parts[a, k].wait_recv()
            total = total + part_recv[a, k].astype(F32)
        hidden[a] = total
        slabs[a, 0] = total.astype(BF16)
        for k in order[:-1]:
            shared[a, k] = send(slabs.at[a, 0], slabs.at[a, k], slab_sems, (a, k), above[k])

    def norm_and_gather(a):
        for k in order[:-1]:
            shared[a, k].wait_recv()
        squares = jnp.zeros((half, 1), F32)
        for k in range(groups):
            value = slabs[a, k].astype(F32)
            squares = squares + jnp.sum(value * value, -1, keepdims=True)
        scale = lax.rsqrt(squares / width + 1e-06)
        for k in range(groups):
            slab_gain = gain_ref[(head - k + groups) % groups]
            rows_all[a, 0, :, k * share : (k + 1) * share] = (
                slabs[a, k].astype(F32) * scale * slab_gain
            ).astype(BF16)
        for q in range(1, chips):
            gathers[a, q] = send(
                rows_all.at[a, 0], rows_all.at[a, q], gather_sems, (a, q), across[q]
            )
        pairs[a, 0] = send(
            rows_all.at[a, 0], rows_all.at[a, chips], pair_sems, (a, 0), partner
        )

    def pass_to_partner(a):
        for q in range(1, chips):
            gathers[a, q].wait_recv()
            pairs[a, q] = send(
                rows_all.at[a, q], rows_all.at[a, chips + q], pair_sems, (a, q), partner
            )

    def take_from_partner(a):
        for q in range(chips):
            pairs[a, q].wait_recv()

    block = min(16, pools)

    def expert_rows(a):
        if a == 0:
            for k in range(groups):
                for e in range(local):
                    loads["gate", (e, k)].wait()
                    loads["up", (e, k)].wait()

        def some_rows(index, carry):
            place = pl.ds(index * block, block)
            gates = rows_all[a, place, :, width:].reshape(block * half, -1).astype(F32)
            lane = lax.broadcasted_iota(jnp.int32, gates.shape, 1)
            for e in range(local):
                gate_part = jnp.zeros((block * half, units), F32)
                up_part = jnp.zeros((block * half, units), F32)
                for k in range(groups):
                    piece = rows_all[a, place, :, k * share : (k + 1) * share].reshape(
                        block * half, share
                    )
                    gate_part += jnp.dot(piece, gate[e, k], preferred_element_type=F32)
                    up_part += jnp.dot(piece, up[e, k], preferred_element_type=F32)
                expert = pool * local + e
                chosen = (lane == expert) | (lane == experts + expert)
                weight = jnp.sum(jnp.where(chosen, gates, 0.0), -1, keepdims=True)
                value = gate_part / (1.0 + jnp.exp(-gate_part)) * up_part * weight
                act[place, :, e * units : (e + 1) * units] = value.astype(BF16).reshape(
                    block, half, units
                )
            return carry

        lax.fori_loop(0, pools // block, some_rows, 0)

    def project_down(a, k):
        if a == 0:
            for e in range(local):
                loads["down", (e, k)].wait()

        def some_rows(index, carry):
            place = pl.ds(index * block, block)
            value = jnp.dot(
                act[place].reshape(block * half, local * units),
                down[k].reshape(local * units, share),
                preferred_element_type=F32,
            )
            produced[a, k, place] = value.astype(BF16).reshape(block, half, share)
            return carry

        lax.fori_loop(0, pools // block, some_rows, 0)
        swaps[a, k] = send(
            produced.at[a, k, pl.ds(chips, chips)],
            pair_recv.at[a, k],
            swap_sems,
            (a, k),
            partner,
        )

    def cross(a, k):
        swaps[a, k].wait_recv()
        for q in range(1, chips):
            produced[a, k, q] = (
                produced[a, k, q].astype(F32) + pair_recv[a, k, q].astype(F32)
            ).astype(BF16)
            planes[a, k, q] = send(
                produced.at[a, k, q],
                plane_recv.at[a, k, q],
                plane_sems,
                (a, k, q),
                across[q],
            )

    def finish(a, k):
        value = produced[a, k, 0].astype(F32) + pair_recv[a, k, 0].astype(F32)
        for q in range(1, chips):
            planes[a, k, q].wait_recv()
            value = value + plane_recv[a, k, q].astype(F32)
        if k:
            last_send[a, k] = value.astype(BF16)
            lasts[a, k] = send(
                last_send.at[a, k], last_recv.at[a, k], last_sems, (a, k), above[k]
            )
        else:
            hidden[a] = hidden[a] + value

    def write(a):
        value = hidden[a]
        for k in order[:-1]:
            lasts[a, k].wait_recv()
            value = value + last_recv[a, k].astype(F32)
        out_ref[a * half : (a + 1) * half, :] = value

    def down_out(a, between):
        for step in range(groups + 1):
            if step < groups:
                project_down(a, order[step])
            else:
                between(step)
            if step:
                cross(a, order[step - 1])
                if step < groups:
                    between(step)

    attend(0)
    pl.semaphore_wait(barrier, len(greeted))
    project_out(0)
    attend(1)
    share_hidden(0)
    project_out(1)
    norm_and_gather(0)
    share_hidden(1)
    norm_and_gather(1)
    pass_to_partner(0)
    take_from_partner(0)
    expert_rows(0)
    down_out(0, lambda step: pass_to_partner(1) if step == groups else None)
    take_from_partner(1)
    expert_rows(1)
    down_out(1, lambda step: finish(0, order[step - 1]))
    for k in order:
        finish(1, k)
    write(0)
    write(1)
    for copy in sent:
        copy.wait_send()


def body(
    x_rows,
    query,
    key_cache,
    value_cache,
    new_key,
    new_value,
    lengths,
    out_proj,
    norm_gain,
    expert_ids,
    gate_weights,
    w_gate,
    w_up,
    w_down,
):
    pools = lax.axis_size("pool")
    groups = lax.axis_size("head")
    rows, width = x_rows.shape
    share = width // groups
    local, _, units = w_gate.shape
    experts = pools * local
    chips = pools // 2
    half = rows // HALVES
    head_size = new_key.shape[1]
    heads = query.shape[1] // head_size
    slots = key_cache.shape[2]
    lanes = -(-2 * experts // 128) * 128
    depth = out_proj.shape[0]
    in_smem = pl.BlockSpec(memory_space=pltpu.SMEM)
    in_vmem = pl.BlockSpec(memory_space=pltpu.VMEM)
    in_hbm = pl.BlockSpec(memory_space=pl.ANY)
    dma = pltpu.SemaphoreType.DMA
    summed = pl.pallas_call(
        functools.partial(layer_kernel, pools, groups, experts),
        out_shape=jax.ShapeDtypeStruct((rows, share), F32),
        in_specs=[in_smem] + [in_vmem] * 7 + [in_hbm] * 6,
        out_specs=in_vmem,
        scratch_shapes=[
            pltpu.VMEM((rows, slots, head_size), BF16),
            pltpu.VMEM((rows, slots, head_size), BF16),
            pltpu.VMEM((rows, heads, head_size), F32),
            pltpu.VMEM((rows, heads, head_size), F32),
            pltpu.VMEM((rows, head_size), F32),
            pltpu.VMEM((rows, head_size), F32),
            pltpu.VMEM((HALVES, half, depth), BF16),
            pltpu.VMEM((groups, depth, share), BF16),
            pltpu.VMEM((local, groups, share, units), BF16),
            pltpu.VMEM((local, groups, share, units), BF16),
            pltpu.VMEM((groups, local, units, share), BF16),
            pltpu.VMEM((HALVES, groups, half, share), BF16),
            pltpu.VMEM((HALVES, groups, half, share), BF16),
            pltpu.VMEM((HALVES, half, share), F32),
            pltpu.VMEM((HALVES, groups, half, share), BF16),
            pltpu.VMEM((HALVES, pools, half, width + lanes), BF16),
            pltpu.VMEM((pools, half, local * units), BF16),
            pltpu.VMEM((HALVES, groups, pools, half, share), BF16),
            pltpu.VMEM((HALVES, groups, chips, half, share), BF16),
            pltpu.VMEM((HALVES, groups, chips, half, share), BF16),
            pltpu.VMEM((HALVES, groups, half, share), BF16),
            pltpu.VMEM((HALVES, groups, half, share), BF16),
            dma((2, rows // TOGETHER)),
            dma((groups * (1 + 3 * local),)),
            dma((2, HALVES, groups)),
            dma((2, HALVES, groups)),
            dma((2, HALVES, chips)),
            dma((2, HALVES, chips)),
            dma((2, HALVES, groups)),
            dma((2, HALVES, groups, chips)),
            dma((2, HALVES, groups)),
        ],
        compiler_params=pltpu.CompilerParams(
            collective_id=0, has_side_effects=True, vmem_limit_bytes=VMEM_BYTES
        ),
    )(
        lengths,
        query,
        new_key,
        new_value,
        x_rows,
        expert_ids.T,
        gate_weights.T,
        norm_gain.reshape(groups, 1, share),
        key_cache,
        value_cache,
        out_proj,
        w_gate,
        w_up,
        w_down,
    )
    return summed.astype(BF16)


def solution(mesh):
    placed = (
        P("pool", None),
        P("pool", "head"),
        P("pool", "head", None, None),
        P("pool", "head", None, None),
        P("pool", "head"),
        P("pool", "head"),
        P("pool"),
        P("head", None),
        P(),
        P("pool", None),
        P("pool", None),
        P("pool", None, "head"),
        P("pool", None, "head"),
        P("pool", "head", None),
    )
    return jax.shard_map(
        body, mesh=mesh, in_specs=placed, out_specs=P("pool", "head"), check_vma=False
    )
```

```python
import functools

import jax
import jax.numpy as jnp
from jax import lax
from jax.experimental import pallas as pl
from jax.experimental.pallas import tpu as pltpu
from jax.sharding import PartitionSpec as P

VMEM_BYTES = 60 * 1024 * 1024
HALVES = 2
TOGETHER = 8

MESH = pl.DeviceIdType.MESH
F32 = jnp.float32
BF16 = jnp.bfloat16


def flip(index, offset, count):
    result, bit = 0, 1
    while bit < count:
        result = result + bit * ((index // bit + offset // bit) % 2)
        bit *= 2
    return result


def layer_kernel(
    pools,
    groups,
    experts,
    lengths_ref,
    query_ref,
    new_key_ref,
    new_value_ref,
    x_ref,
    ids_ref,
    gate_weight_ref,
    gain_ref,
    key_hbm,
    value_hbm,
    proj_hbm,
    gate_hbm,
    up_hbm,
    down_hbm,
    out_ref,
    keys,
    values,
    query_heads,
    mixed_heads,
    fresh_keys,
    fresh_values,
    attn,
    proj,
    gate,
    up,
    down,
    part_send,
    part_recv,
    hidden,
    slabs,
    rows_all,
    act,
    produced,
    pair_recv,
    plane_recv,
    last_send,
    last_recv,
    cache_sem,
    load_sem,
    part_sems,
    slab_sems,
    gather_sems,
    pair_sems,
    swap_sems,
    plane_sems,
    last_sems,
):
    chips = pools // 2
    half, share = hidden.shape[1:]
    width = groups * share
    local = gate.shape[0]
    units = gate.shape[3]
    lanes = rows_all.shape[3] - width
    heads, head_size = query_heads.shape[1:]
    slots = keys.shape[1]
    pool, head = lax.axis_index("pool"), lax.axis_index("head")
    chip, core = pool // 2, pool % 2
    partner = {"pool": chip * 2 + 1 - core}
    above = [{"head": (head + k) % groups} for k in range(groups)]
    across = [{"pool": flip(chip, q, chips) * 2 + core} for q in range(chips)]
    order = list(range(1, groups)) + [0]
    sent = []

    def send(source, target, sems, place, device):
        copy = pltpu.make_async_remote_copy(
            src_ref=source,
            dst_ref=target,
            send_sem=sems.at[(0,) + place],
            recv_sem=sems.at[(1,) + place],
            device_id=device,
            device_id_type=MESH,
        )
        copy.start()
        sent.append(copy)
        return copy

    loads = {}

    def load(name, index, source, target):
        copy = pltpu.make_async_copy(source, target, load_sem.at[len(loads)])
        copy.start()
        loads[name, index] = copy

    def columns(k):
        return pl.ds(pl.multiple_of((head + k) % groups * share, share), share)

    def depths(k):
        return pl.ds(pl.multiple_of((head - k + groups) % groups * share, share), share)

    def cache_copies(index):
        place = pl.ds(index * TOGETHER, TOGETHER)
        return [
            pltpu.make_async_copy(key_hbm.at[place, 0], keys.at[place], cache_sem.at[0, index]),
            pltpu.make_async_copy(
                value_hbm.at[place, 0], values.at[place], cache_sem.at[1, index]
            ),
        ]

    blocks = half // TOGETHER

    def load_cache(a):
        for index in range(a * blocks, (a + 1) * blocks):
            for copy in cache_copies(index):
                copy.start()

    load_cache(0)

    def load_projection():
        for k in order:
            load("proj", k, proj_hbm.at[:, columns(k)], proj.at[k])

    def load_inward():
        for k in range(groups):
            for e in range(local):
                load("gate", (e, k), gate_hbm.at[e, depths(k)], gate.at[e, k])
                load("up", (e, k), up_hbm.at[e, depths(k)], up.at[e, k])

    def load_down():
        for k in order:
            for e in range(local):
                load("down", (e, k), down_hbm.at[e, :, columns(k)], down.at[k, e])

    barrier = pltpu.get_barrier_semaphore()
    greeted = above[1:] + across[1:] + [partner]
    for device in greeted:
        pl.semaphore_signal(barrier, inc=1, device_id=device, device_id_type=MESH)

    for i in range(heads):
        query_heads[:, i, :] = query_ref[:, i * head_size : (i + 1) * head_size].astype(F32)
    fresh_keys[...] = new_key_ref[...].astype(F32)
    fresh_values[...] = new_value_ref[...].astype(F32)
    score_scale = head_size ** (-0.5)

    rows = HALVES * half
    lane = lax.broadcasted_iota(jnp.int32, (lanes, rows), 0)
    named = jnp.where(lane < experts, lane, lane - experts)
    table = jnp.zeros((lanes, rows), F32)
    for i in range(ids_ref.shape[0]):
        table += jnp.where(ids_ref[i : i + 1, :] == named, gate_weight_ref[i : i + 1, :], 0.0)
    first = table.astype(BF16).astype(F32)
    terms = jnp.where(lane < experts, first, table - first).astype(BF16)
    square = (rows, rows)
    eye = lax.broadcasted_iota(jnp.int32, square, 0) == lax.broadcasted_iota(jnp.int32, square, 1)
    terms = lax.dot_general(
        eye.astype(F32).astype(BF16), terms, (((1,), (1,)), ((), ())), preferred_element_type=F32
    ).astype(BF16)
    for a in range(HALVES):
        rows_all[a, 0, :, width:] = terms[a * half : (a + 1) * half]

    def attend(a):
        def requests(index, carry):
            for copy in cache_copies(index):
                copy.wait()
            place = lax.broadcasted_iota(jnp.int32, (heads, slots), 1)
            numbers = [index * TOGETHER + i for i in range(TOGETHER)]
            queries = [query_heads[r] for r in numbers]
            scores = [
                lax.dot_general(
                    query.astype(BF16),
                    keys[r],
                    (((1,), (1,)), ((), ())),
                    preferred_element_type=F32,
                )
                for r, query in zip(numbers, queries)
            ]
            scores = [
                jnp.where(place < lengths_ref[r], score * score_scale, -1e30)
                for r, score in zip(numbers, scores)
            ]
            fresh = [
                jnp.sum(query * fresh_keys[pl.ds(r, 1)], -1, keepdims=True) * score_scale
                for r, query in zip(numbers, queries)
            ]
            highest = [
                jnp.maximum(jnp.max(score, -1, keepdims=True), new)
                for score, new in zip(scores, fresh)
            ]
            weights = [jnp.exp(score - top) for score, top in zip(scores, highest)]
            mixed = [
                jnp.dot(weight.astype(BF16), values[r], preferred_element_type=F32)
                for r, weight in zip(numbers, weights)
            ]
            own = [jnp.exp(new - top) for new, top in zip(fresh, highest)]
            totals = [
                jnp.sum(weight, -1, keepdims=True) + new for weight, new in zip(weights, own)
            ]
            mixed = [
                (value + new * fresh_values[pl.ds(r, 1)]) / total
                for r, value, new, total in zip(numbers, mixed, own, totals)
            ]
            for r, value in zip(numbers, mixed):
                mixed_heads[r] = value
            return carry

        lax.fori_loop(a * blocks, (a + 1) * blocks, requests, 0)
        place = slice(a * half, (a + 1) * half)
        for i in range(heads):
            attn[a, :, i * head_size : (i + 1) * head_size] = mixed_heads[place, i, :].astype(BF16)

    parts, shared, gathers, pairs, swaps, planes, lasts = {}, {}, {}, {}, {}, {}, {}

    def project_out(a):
        for k in order:
            if a == 0:
                loads["proj", k].wait()
            term = jnp.dot(attn[a], proj[k], preferred_element_type=F32)
            if k:
                part_send[a, k] = term.astype(BF16)
                parts[a, k] = send(
                    part_send.at[a, k], part_recv.at[a, k], part_sems, (a, k), above[k]
                )
            else:
                own = pl.ds(pl.multiple_of(head * share, share), share)
                hidden[a] = term + x_ref[a * half : (a + 1) * half, own].astype(F32)

    def share_hidden(a):
        total = hidden[a]
        for k in order[:-1]:
            parts[a, k].wait_recv()
            total = total + part_recv[a, k].astype(F32)
        hidden[a] = total
        slabs[a, 0] = total.astype(BF16)
        for k in order[:-1]:
            shared[a, k] = send(slabs.at[a, 0], slabs.at[a, k], slab_sems, (a, k), above[k])

    def norm_and_gather(a):
        for k in order[:-1]:
            shared[a, k].wait_recv()
        squares = jnp.zeros((half, 1), F32)
        for k in range(groups):
            value = slabs[a, k].astype(F32)
            squares = squares + jnp.sum(value * value, -1, keepdims=True)
        scale = lax.rsqrt(squares / width + 1e-06)
        for k in range(groups):
            slab_gain = gain_ref[(head - k + groups) % groups]
            rows_all[a, 0, :, k * share : (k + 1) * share] = (
                slabs[a, k].astype(F32) * scale * slab_gain
            ).astype(BF16)
        for q in range(1, chips):
            gathers[a, q] = send(
                rows_all.at[a, 0], rows_all.at[a, q], gather_sems, (a, q), across[q]
            )
        pairs[a, 0] = send(
            rows_all.at[a, 0], rows_all.at[a, chips], pair_sems, (a, 0), partner
        )

    def pass_to_partner(a):
        for q in range(1, chips):
            gathers[a, q].wait_recv()
            pairs[a, q] = send(
                rows_all.at[a, q], rows_all.at[a, chips + q], pair_sems, (a, q), partner
            )

    def take_from_partner(a):
        for q in range(chips):
            pairs[a, q].wait_recv()

    block = min(16, pools)

    def expert_rows(a):
        if a == 0:
            for k in range(groups):
                for e in range(local):
                    loads["gate", (e, k)].wait()
                    loads["up", (e, k)].wait()

        def some_rows(index, carry):
            place = pl.ds(index * block, block)
            gates = rows_all[a, place, :, width:].reshape(block * half, -1).astype(F32)
            lane = lax.broadcasted_iota(jnp.int32, gates.shape, 1)
            for e in range(local):
                gate_part = jnp.zeros((block * half, units), F32)
                up_part = jnp.zeros((block * half, units), F32)
                for k in range(groups):
                    piece = rows_all[a, place, :, k * share : (k + 1) * share].reshape(
                        block * half, share
                    )
                    gate_part += jnp.dot(piece, gate[e, k], preferred_element_type=F32)
                    up_part += jnp.dot(piece, up[e, k], preferred_element_type=F32)
                expert = pool * local + e
                chosen = (lane == expert) | (lane == experts + expert)
                weight = jnp.sum(jnp.where(chosen, gates, 0.0), -1, keepdims=True)
                value = gate_part / (1.0 + jnp.exp(-gate_part)) * up_part * weight
                act[place, :, e * units : (e + 1) * units] = value.astype(BF16).reshape(
                    block, half, units
                )
            return carry

        lax.fori_loop(0, pools // block, some_rows, 0)

    def project_down(a, k):
        if a == 0:
            for e in range(local):
                loads["down", (e, k)].wait()

        def some_rows(index, carry):
            place = pl.ds(index * block, block)
            value = jnp.dot(
                act[place].reshape(block * half, local * units),
                down[k].reshape(local * units, share),
                preferred_element_type=F32,
            )
            produced[a, k, place] = value.astype(BF16).reshape(block, half, share)
            return carry

        lax.fori_loop(0, pools // block, some_rows, 0)
        swaps[a, k] = send(
            produced.at[a, k, pl.ds(chips, chips)],
            pair_recv.at[a, k],
            swap_sems,
            (a, k),
            partner,
        )

    def cross(a, k):
        swaps[a, k].wait_recv()
        for q in range(1, chips):
            produced[a, k, q] = (
                produced[a, k, q].astype(F32) + pair_recv[a, k, q].astype(F32)
            ).astype(BF16)
            planes[a, k, q] = send(
                produced.at[a, k, q],
                plane_recv.at[a, k, q],
                plane_sems,
                (a, k, q),
                across[q],
            )

    def finish(a, k):
        value = produced[a, k, 0].astype(F32) + pair_recv[a, k, 0].astype(F32)
        for q in range(1, chips):
            planes[a, k, q].wait_recv()
            value = value + plane_recv[a, k, q].astype(F32)
        if k:
            last_send[a, k] = value.astype(BF16)
            lasts[a, k] = send(
                last_send.at[a, k], last_recv.at[a, k], last_sems, (a, k), above[k]
            )
        else:
            hidden[a] = hidden[a] + value

    def write(a):
        value = hidden[a]
        for k in order[:-1]:
            lasts[a, k].wait_recv()
            value = value + last_recv[a, k].astype(F32)
        out_ref[a * half : (a + 1) * half, :] = value

    def down_out(a, between):
        for step in range(groups + 2):
            if step < groups:
                project_down(a, order[step])
            else:
                between(step - 2)
            if step >= 2:
                cross(a, order[step - 2])
                if step < groups:
                    between(step - 2)

    load_projection()
    attend(0)
    for a in range(1, HALVES):
        load_cache(a)
    pl.semaphore_wait(barrier, len(greeted))
    project_out(0)
    load_inward()
    attend(1)
    load_down()
    share_hidden(0)
    project_out(1)
    norm_and_gather(0)
    share_hidden(1)
    norm_and_gather(1)
    pass_to_partner(0)
    take_from_partner(0)
    expert_rows(0)
    down_out(0, lambda step: pass_to_partner(1) if step == groups - 1 else None)
    take_from_partner(1)
    expert_rows(1)
    down_out(1, lambda step: finish(0, order[step]))
    for k in order[:-1]:
        finish(1, k)
    write(0)
    finish(1, 0)
    write(1)
    for copy in sent:
        copy.wait_send()


def body(
    x_rows,
    query,
    key_cache,
    value_cache,
    new_key,
    new_value,
    lengths,
    out_proj,
    norm_gain,
    expert_ids,
    gate_weights,
    w_gate,
    w_up,
    w_down,
):
    pools = lax.axis_size("pool")
    groups = lax.axis_size("head")
    rows, width = x_rows.shape
    share = width // groups
    local, _, units = w_gate.shape
    experts = pools * local
    chips = pools // 2
    half = rows // HALVES
    head_size = new_key.shape[1]
    heads = query.shape[1] // head_size
    slots = key_cache.shape[2]
    lanes = -(-2 * experts // 128) * 128
    depth = out_proj.shape[0]
    in_smem = pl.BlockSpec(memory_space=pltpu.SMEM)
    in_vmem = pl.BlockSpec(memory_space=pltpu.VMEM)
    in_hbm = pl.BlockSpec(memory_space=pl.ANY)
    dma = pltpu.SemaphoreType.DMA
    summed = pl.pallas_call(
        functools.partial(layer_kernel, pools, groups, experts),
        out_shape=jax.ShapeDtypeStruct((rows, share), F32),
        in_specs=[in_smem] + [in_vmem] * 7 + [in_hbm] * 6,
        out_specs=in_vmem,
        scratch_shapes=[
            pltpu.VMEM((rows, slots, head_size), BF16),
            pltpu.VMEM((rows, slots, head_size), BF16),
            pltpu.VMEM((rows, heads, head_size), F32),
            pltpu.VMEM((rows, heads, head_size), F32),
            pltpu.VMEM((rows, head_size), F32),
            pltpu.VMEM((rows, head_size), F32),
            pltpu.VMEM((HALVES, half, depth), BF16),
            pltpu.VMEM((groups, depth, share), BF16),
            pltpu.VMEM((local, groups, share, units), BF16),
            pltpu.VMEM((local, groups, share, units), BF16),
            pltpu.VMEM((groups, local, units, share), BF16),
            pltpu.VMEM((HALVES, groups, half, share), BF16),
            pltpu.VMEM((HALVES, groups, half, share), BF16),
            pltpu.VMEM((HALVES, half, share), F32),
            pltpu.VMEM((HALVES, groups, half, share), BF16),
            pltpu.VMEM((HALVES, pools, half, width + lanes), BF16),
            pltpu.VMEM((pools, half, local * units), BF16),
            pltpu.VMEM((HALVES, groups, pools, half, share), BF16),
            pltpu.VMEM((HALVES, groups, chips, half, share), BF16),
            pltpu.VMEM((HALVES, groups, chips, half, share), BF16),
            pltpu.VMEM((HALVES, groups, half, share), BF16),
            pltpu.VMEM((HALVES, groups, half, share), BF16),
            dma((2, rows // TOGETHER)),
            dma((groups * (1 + 3 * local),)),
            dma((2, HALVES, groups)),
            dma((2, HALVES, groups)),
            dma((2, HALVES, chips)),
            dma((2, HALVES, chips)),
            dma((2, HALVES, groups)),
            dma((2, HALVES, groups, chips)),
            dma((2, HALVES, groups)),
        ],
        compiler_params=pltpu.CompilerParams(
            collective_id=0, has_side_effects=True, vmem_limit_bytes=VMEM_BYTES
        ),
    )(
        lengths,
        query,
        new_key,
        new_value,
        x_rows,
        expert_ids.T,
        gate_weights.T,
        norm_gain.reshape(groups, 1, share),
        key_cache,
        value_cache,
        out_proj,
        w_gate,
        w_up,
        w_down,
    )
    return summed.astype(BF16)


def solution(mesh):
    placed = (
        P("pool", None),
        P("pool", "head"),
        P("pool", "head", None, None),
        P("pool", "head", None, None),
        P("pool", "head"),
        P("pool", "head"),
        P("pool"),
        P("head", None),
        P(),
        P("pool", None),
        P("pool", None),
        P("pool", None, "head"),
        P("pool", None, "head"),
        P("pool", "head", None),
    )
    return jax.shard_map(
        body, mesh=mesh, in_specs=placed, out_specs=P("pool", "head"), check_vma=False
    )
```

```python
import functools

import jax
import jax.numpy as jnp
from jax import lax
from jax.experimental import pallas as pl
from jax.experimental.pallas import tpu as pltpu
from jax.sharding import PartitionSpec as P

VMEM_BYTES = 60 * 1024 * 1024
HALVES = 2
TOGETHER = 8

MESH = pl.DeviceIdType.MESH
F32 = jnp.float32
BF16 = jnp.bfloat16


def flip(index, offset, count):
    result, bit = 0, 1
    while bit < count:
        result = result + bit * ((index // bit + offset // bit) % 2)
        bit *= 2
    return result


def layer_kernel(
    pools,
    groups,
    experts,
    lengths_ref,
    query_ref,
    new_key_ref,
    new_value_ref,
    x_ref,
    ids_ref,
    gate_weight_ref,
    gain_ref,
    key_hbm,
    value_hbm,
    proj_hbm,
    gate_hbm,
    up_hbm,
    down_hbm,
    out_ref,
    keys,
    values,
    query_heads,
    mixed_heads,
    fresh_keys,
    fresh_values,
    attn,
    proj,
    gate,
    up,
    down,
    part_send,
    part_recv,
    hidden,
    slabs,
    rows_all,
    act,
    produced,
    pair_recv,
    plane_recv,
    last_send,
    last_recv,
    cache_sem,
    load_sem,
    part_sems,
    slab_sems,
    gather_sems,
    pair_sems,
    swap_sems,
    plane_sems,
    last_sems,
):
    chips = pools // 2
    half, share = hidden.shape[1:]
    width = groups * share
    local = gate.shape[0]
    units = gate.shape[3]
    lanes = rows_all.shape[3] - width
    heads, head_size = query_heads.shape[1:]
    slots = keys.shape[1]
    pool, head = lax.axis_index("pool"), lax.axis_index("head")
    chip, core = pool // 2, pool % 2
    partner = {"pool": chip * 2 + 1 - core}
    above = [{"head": (head + k) % groups} for k in range(groups)]
    across = [{"pool": flip(chip, q, chips) * 2 + core} for q in range(chips)]
    order = list(range(1, groups)) + [0]
    sent = []

    def send(source, target, sems, place, device):
        copy = pltpu.make_async_remote_copy(
            src_ref=source,
            dst_ref=target,
            send_sem=sems.at[(0,) + place],
            recv_sem=sems.at[(1,) + place],
            device_id=device,
            device_id_type=MESH,
        )
        copy.start()
        sent.append(copy)
        return copy

    loads = {}

    def load(name, index, source, target):
        copy = pltpu.make_async_copy(source, target, load_sem.at[len(loads)])
        copy.start()
        loads[name, index] = copy

    def columns(k):
        return pl.ds(pl.multiple_of((head + k) % groups * share, share), share)

    def depths(k):
        return pl.ds(pl.multiple_of((head - k + groups) % groups * share, share), share)

    def cache_copies(index):
        place = pl.ds(index * TOGETHER, TOGETHER)
        return [
            pltpu.make_async_copy(key_hbm.at[place, 0], keys.at[place], cache_sem.at[0, index]),
            pltpu.make_async_copy(
                value_hbm.at[place, 0], values.at[place], cache_sem.at[1, index]
            ),
        ]

    blocks = half // TOGETHER

    def load_cache(a):
        for index in range(a * blocks, (a + 1) * blocks):
            for copy in cache_copies(index):
                copy.start()

    load_cache(0)

    def load_projection():
        for k in order:
            load("proj", k, proj_hbm.at[:, columns(k)], proj.at[k])

    def load_inward():
        for k in range(groups):
            for e in range(local):
                load("gate", (e, k), gate_hbm.at[e, depths(k)], gate.at[e, k])
                load("up", (e, k), up_hbm.at[e, depths(k)], up.at[e, k])

    def load_down():
        for k in order:
            for e in range(local):
                load("down", (e, k), down_hbm.at[e, :, columns(k)], down.at[k, e])

    barrier = pltpu.get_barrier_semaphore()
    greeted = above[1:] + across[1:] + [partner]
    for device in greeted:
        pl.semaphore_signal(barrier, inc=1, device_id=device, device_id_type=MESH)

    for i in range(heads):
        query_heads[:, i, :] = query_ref[:, i * head_size : (i + 1) * head_size].astype(F32)
    fresh_keys[...] = new_key_ref[...].astype(F32)
    fresh_values[...] = new_value_ref[...].astype(F32)
    score_scale = head_size ** (-0.5)

    rows = HALVES * half
    lane = lax.broadcasted_iota(jnp.int32, (lanes, rows), 0)
    named = jnp.where(lane < experts, lane, lane - experts)
    table = jnp.zeros((lanes, rows), F32)
    for i in range(ids_ref.shape[0]):
        table += jnp.where(ids_ref[i : i + 1, :] == named, gate_weight_ref[i : i + 1, :], 0.0)
    first = table.astype(BF16).astype(F32)
    terms = jnp.where(lane < experts, first, table - first).astype(BF16)
    square = (rows, rows)
    eye = lax.broadcasted_iota(jnp.int32, square, 0) == lax.broadcasted_iota(jnp.int32, square, 1)
    terms = lax.dot_general(
        eye.astype(F32).astype(BF16), terms, (((1,), (1,)), ((), ())), preferred_element_type=F32
    ).astype(BF16)
    for a in range(HALVES):
        rows_all[a, 0, :, width:] = terms[a * half : (a + 1) * half]

    def attend(a):
        def requests(index, carry):
            for copy in cache_copies(index):
                copy.wait()
            place = lax.broadcasted_iota(jnp.int32, (heads, slots), 1)
            numbers = [index * TOGETHER + i for i in range(TOGETHER)]
            queries = [query_heads[r] for r in numbers]
            scores = [
                lax.dot_general(
                    query.astype(BF16),
                    keys[r],
                    (((1,), (1,)), ((), ())),
                    preferred_element_type=F32,
                )
                for r, query in zip(numbers, queries)
            ]
            scores = [
                jnp.where(place < lengths_ref[r], score * score_scale, -1e30)
                for r, score in zip(numbers, scores)
            ]
            fresh = [
                jnp.sum(query * fresh_keys[pl.ds(r, 1)], -1, keepdims=True) * score_scale
                for r, query in zip(numbers, queries)
            ]
            highest = [
                jnp.maximum(jnp.max(score, -1, keepdims=True), new)
                for score, new in zip(scores, fresh)
            ]
            weights = [jnp.exp(score - top) for score, top in zip(scores, highest)]
            mixed = [
                jnp.dot(weight.astype(BF16), values[r], preferred_element_type=F32)
                for r, weight in zip(numbers, weights)
            ]
            own = [jnp.exp(new - top) for new, top in zip(fresh, highest)]
            totals = [
                jnp.sum(weight, -1, keepdims=True) + new for weight, new in zip(weights, own)
            ]
            mixed = [
                (value + new * fresh_values[pl.ds(r, 1)]) / total
                for r, value, new, total in zip(numbers, mixed, own, totals)
            ]
            for r, value in zip(numbers, mixed):
                mixed_heads[r] = value
            return carry

        lax.fori_loop(a * blocks, (a + 1) * blocks, requests, 0)
        place = slice(a * half, (a + 1) * half)
        for i in range(heads):
            attn[a, :, i * head_size : (i + 1) * head_size] = mixed_heads[place, i, :].astype(BF16)

    parts, shared, gathers, pairs, swaps, planes, lasts = {}, {}, {}, {}, {}, {}, {}

    def project_out(a):
        for k in order:
            if a == 0:
                loads["proj", k].wait()
            term = jnp.dot(attn[a], proj[k], preferred_element_type=F32)
            if k:
                part_send[a, k] = term.astype(BF16)
                parts[a, k] = send(
                    part_send.at[a, k], part_recv.at[a, k], part_sems, (a, k), above[k]
                )
            else:
                own = pl.ds(pl.multiple_of(head * share, share), share)
                hidden[a] = term + x_ref[a * half : (a + 1) * half, own].astype(F32)

    def share_hidden(a):
        total = hidden[a]
        for k in order[:-1]:
            parts[a, k].wait_recv()
            total = total + part_recv[a, k].astype(F32)
        hidden[a] = total
        slabs[a, 0] = total.astype(BF16)
        for k in order[:-1]:
            shared[a, k] = send(slabs.at[a, 0], slabs.at[a, k], slab_sems, (a, k), above[k])

    def norm_and_gather(a):
        for k in order[:-1]:
            shared[a, k].wait_recv()
        squares = jnp.zeros((half, 1), F32)
        for k in range(groups):
            value = slabs[a, k].astype(F32)
            squares = squares + jnp.sum(value * value, -1, keepdims=True)
        scale = lax.rsqrt(squares / width + 1e-06)
        for k in range(groups):
            slab_gain = gain_ref[(head - k + groups) % groups]
            rows_all[a, 0, :, k * share : (k + 1) * share] = (
                slabs[a, k].astype(F32) * scale * slab_gain
            ).astype(BF16)
        for q in range(1, chips):
            gathers[a, q] = send(
                rows_all.at[a, 0], rows_all.at[a, q], gather_sems, (a, q), across[q]
            )
        pairs[a, 0] = send(
            rows_all.at[a, 0], rows_all.at[a, chips], pair_sems, (a, 0), partner
        )

    def pass_to_partner(a):
        for q in range(1, chips):
            gathers[a, q].wait_recv()
            pairs[a, q] = send(
                rows_all.at[a, q], rows_all.at[a, chips + q], pair_sems, (a, q), partner
            )

    def take_from_partner(a):
        for q in range(chips):
            pairs[a, q].wait_recv()

    block = min(16, pools)

    def over_blocks(work):
        if pools == block:
            work(0, 0)
        else:
            lax.fori_loop(0, pools // block, work, 0)

    def expert_rows(a):
        if a == 0:
            for k in range(groups):
                for e in range(local):
                    loads["gate", (e, k)].wait()
                    loads["up", (e, k)].wait()

        def some_rows(index, carry):
            place = pl.ds(index * block, block)
            gates = rows_all[a, place, :, width:].reshape(block * half, -1).astype(F32)
            lane = lax.broadcasted_iota(jnp.int32, gates.shape, 1)
            for e in range(local):
                gate_part = jnp.zeros((block * half, units), F32)
                up_part = jnp.zeros((block * half, units), F32)
                for k in range(groups):
                    piece = rows_all[a, place, :, k * share : (k + 1) * share].reshape(
                        block * half, share
                    )
                    gate_part += jnp.dot(piece, gate[e, k], preferred_element_type=F32)
                    up_part += jnp.dot(piece, up[e, k], preferred_element_type=F32)
                expert = pool * local + e
                chosen = (lane == expert) | (lane == experts + expert)
                weight = jnp.sum(jnp.where(chosen, gates, 0.0), -1, keepdims=True)
                value = gate_part / (1.0 + jnp.exp(-gate_part)) * up_part * weight
                act[place, :, e * units : (e + 1) * units] = value.astype(BF16).reshape(
                    block, half, units
                )
            return carry

        over_blocks(some_rows)

    def project_down(a, k):
        if a == 0:
            for e in range(local):
                loads["down", (e, k)].wait()

        def some_rows(index, carry):
            place = pl.ds(index * block, block)
            value = jnp.dot(
                act[place].reshape(block * half, local * units),
                down[k].reshape(local * units, share),
                preferred_element_type=F32,
            )
            produced[a, k, place] = value.astype(BF16).reshape(block, half, share)
            return carry

        over_blocks(some_rows)
        swaps[a, k] = send(
            produced.at[a, k, pl.ds(chips, chips)],
            pair_recv.at[a, k],
            swap_sems,
            (a, k),
            partner,
        )

    def cross(a, k):
        swaps[a, k].wait_recv()
        for q in range(1, chips):
            produced[a, k, q] = (
                produced[a, k, q].astype(F32) + pair_recv[a, k, q].astype(F32)
            ).astype(BF16)
            planes[a, k, q] = send(
                produced.at[a, k, q],
                plane_recv.at[a, k, q],
                plane_sems,
                (a, k, q),
                across[q],
            )

    def finish(a, k):
        value = produced[a, k, 0].astype(F32) + pair_recv[a, k, 0].astype(F32)
        for q in range(1, chips):
            planes[a, k, q].wait_recv()
            value = value + plane_recv[a, k, q].astype(F32)
        if k:
            last_send[a, k] = value.astype(BF16)
            lasts[a, k] = send(
                last_send.at[a, k], last_recv.at[a, k], last_sems, (a, k), above[k]
            )
        else:
            hidden[a] = hidden[a] + value

    def write(a):
        value = hidden[a]
        for k in order[:-1]:
            lasts[a, k].wait_recv()
            value = value + last_recv[a, k].astype(F32)
        out_ref[a * half : (a + 1) * half, :] = value

    def down_out(a, between):
        for step in range(groups + 2):
            if step < groups:
                project_down(a, order[step])
            else:
                between(step - 2)
            if step >= 2:
                cross(a, order[step - 2])
                if step < groups:
                    between(step - 2)

    load_projection()
    attend(0)
    for a in range(1, HALVES):
        load_cache(a)
    pl.semaphore_wait(barrier, len(greeted))
    project_out(0)
    load_inward()
    attend(1)
    load_down()
    share_hidden(0)
    project_out(1)
    norm_and_gather(0)
    share_hidden(1)
    norm_and_gather(1)
    pass_to_partner(0)
    take_from_partner(0)
    expert_rows(0)
    down_out(0, lambda step: pass_to_partner(1) if step == groups - 1 else None)
    take_from_partner(1)
    expert_rows(1)
    down_out(1, lambda step: finish(0, order[step]))
    for k in order[:-1]:
        finish(1, k)
    write(0)
    finish(1, 0)
    write(1)
    for copy in sent:
        copy.wait_send()


def body(
    x_rows,
    query,
    key_cache,
    value_cache,
    new_key,
    new_value,
    lengths,
    out_proj,
    norm_gain,
    expert_ids,
    gate_weights,
    w_gate,
    w_up,
    w_down,
):
    pools = lax.axis_size("pool")
    groups = lax.axis_size("head")
    rows, width = x_rows.shape
    share = width // groups
    local, _, units = w_gate.shape
    experts = pools * local
    chips = pools // 2
    half = rows // HALVES
    head_size = new_key.shape[1]
    heads = query.shape[1] // head_size
    slots = key_cache.shape[2]
    lanes = -(-2 * experts // 128) * 128
    depth = out_proj.shape[0]
    in_smem = pl.BlockSpec(memory_space=pltpu.SMEM)
    in_vmem = pl.BlockSpec(memory_space=pltpu.VMEM)
    in_hbm = pl.BlockSpec(memory_space=pl.ANY)
    dma = pltpu.SemaphoreType.DMA
    summed = pl.pallas_call(
        functools.partial(layer_kernel, pools, groups, experts),
        out_shape=jax.ShapeDtypeStruct((rows, share), F32),
        in_specs=[in_smem] + [in_vmem] * 7 + [in_hbm] * 6,
        out_specs=in_vmem,
        scratch_shapes=[
            pltpu.VMEM((rows, slots, head_size), BF16),
            pltpu.VMEM((rows, slots, head_size), BF16),
            pltpu.VMEM((rows, heads, head_size), F32),
            pltpu.VMEM((rows, heads, head_size), F32),
            pltpu.VMEM((rows, head_size), F32),
            pltpu.VMEM((rows, head_size), F32),
            pltpu.VMEM((HALVES, half, depth), BF16),
            pltpu.VMEM((groups, depth, share), BF16),
            pltpu.VMEM((local, groups, share, units), BF16),
            pltpu.VMEM((local, groups, share, units), BF16),
            pltpu.VMEM((groups, local, units, share), BF16),
            pltpu.VMEM((HALVES, groups, half, share), BF16),
            pltpu.VMEM((HALVES, groups, half, share), BF16),
            pltpu.VMEM((HALVES, half, share), F32),
            pltpu.VMEM((HALVES, groups, half, share), BF16),
            pltpu.VMEM((HALVES, pools, half, width + lanes), BF16),
            pltpu.VMEM((pools, half, local * units), BF16),
            pltpu.VMEM((HALVES, groups, pools, half, share), BF16),
            pltpu.VMEM((HALVES, groups, chips, half, share), BF16),
            pltpu.VMEM((HALVES, groups, chips, half, share), BF16),
            pltpu.VMEM((HALVES, groups, half, share), BF16),
            pltpu.VMEM((HALVES, groups, half, share), BF16),
            dma((2, rows // TOGETHER)),
            dma((groups * (1 + 3 * local),)),
            dma((2, HALVES, groups)),
            dma((2, HALVES, groups)),
            dma((2, HALVES, chips)),
            dma((2, HALVES, chips)),
            dma((2, HALVES, groups)),
            dma((2, HALVES, groups, chips)),
            dma((2, HALVES, groups)),
        ],
        compiler_params=pltpu.CompilerParams(
            collective_id=0, has_side_effects=True, vmem_limit_bytes=VMEM_BYTES
        ),
    )(
        lengths,
        query,
        new_key,
        new_value,
        x_rows,
        expert_ids.T,
        gate_weights.T,
        norm_gain.reshape(groups, 1, share),
        key_cache,
        value_cache,
        out_proj,
        w_gate,
        w_up,
        w_down,
    )
    return summed.astype(BF16)


def solution(mesh):
    placed = (
        P("pool", None),
        P("pool", "head"),
        P("pool", "head", None, None),
        P("pool", "head", None, None),
        P("pool", "head"),
        P("pool", "head"),
        P("pool"),
        P("head", None),
        P(),
        P("pool", None),
        P("pool", None),
        P("pool", None, "head"),
        P("pool", None, "head"),
        P("pool", "head", None),
    )
    return jax.shard_map(
        body, mesh=mesh, in_specs=placed, out_specs=P("pool", "head"), check_vma=False
    )
```
